512 devices in a mesh: rows: 8 (over z), vocab: 16 (over y, core), mp: 4 (over x).
Axes of the slice: x: 4, y: 8, z: 8, core: 2. Of those that a mesh axis runs over, the one named last changes fastest.
Arguments:
- hidden: bfloat16 [2, 32768, 5120], P(None, ('rows', 'vocab'), 'mp'), may hold values from -2 to 2
- gain: bfloat16 [5120], replicated, may hold values from 0.5 to 1.5
- head: bfloat16 [5120, 32000], P('rows', ('vocab', 'mp')), may hold values from -0.36336105 to 0.36336105
- exit_slots: int32 [2, 768], P(None, ('rows', 'vocab')), may hold values from 0 to 256, as said below
- targets: int32 [32768], P(('rows', 'vocab')), may hold values from 0 to 31999
Outputs:
- exit_grads: bfloat16 [2, 768, 5120], P(None, ('rows', 'vocab'), 'mp')
- group_loss: float32 [2, 8], P(None, 'rows')
The draws below stay inside these ranges and needn't reach their ends.
Inputs may be any that keep to these rules, and one draw needn't show every extreme that they name: `exit_slots`: each block of 6 entries (one layer, one device of rows+vocab) starts with its live entries, distinct local rows below 256; all its other entries equal 256. In each layer the 16 blocks of one index of rows hold exactly 36 live entries together, and one of them holds 6.
All inputs are finite; a program needn't handle non-finite values.
Results may differ from the reference program's by a relative error of at most 0.014.
Values may be sent and summed in bfloat16 or wider, within the bound.
No kernel may reach another device: no remote copies, remote signals or barrier semaphores. Data moves between devices by JAX's collectives and lax.ppermute only.
A program may use at most 64 MiB of HBM per device.

```python
import math
import jax
import jax.numpy as jnp
import numpy as np
from jax import lax

D = 5120
VOCAB = 32000
LAYERS = 2
ROW_DEV = 256
EXIT_MOST = 6
GROUP_EXIT = 36
ROWS = 32768
SLOTS = 768
N_ROWS = 8
N_VOCAB = 16


def exit_plan(key):
    key = jax.random.fold_in(key, 17)
    key_heavy, key_score, key_rows = jax.random.split(key, 3)
    groups = LAYERS * N_ROWS
    pool = N_VOCAB * EXIT_MOST
    devices_rv = N_ROWS * N_VOCAB
    heavy = jax.random.randint(key_heavy, (groups, 1), 0, N_VOCAB)
    slot_ids = jnp.arange(pool, dtype=jnp.int32)
    owner = slot_ids // EXIT_MOST
    noise = jax.random.randint(key_score, (groups, pool), 0, 4096)
    scores = (noise + 4096 * owner[None, :] // N_VOCAB) * pool + slot_ids[None, :]
    scores = jnp.where(owner[None, :] == heavy, -1 - slot_ids[None, :], scores)
    _, chosen = lax.top_k(scores, GROUP_EXIT - EXIT_MOST)
    marked = jnp.sum(jax.nn.one_hot(chosen, pool, dtype=jnp.int32), axis=1)
    counts = jnp.sum(marked.reshape(groups, N_VOCAB, EXIT_MOST), axis=2)
    counts = counts + EXIT_MOST * (jnp.arange(N_VOCAB, dtype=jnp.int32)[None, :] == heavy).astype(jnp.int32)
    counts = counts.reshape(LAYERS, devices_rv)
    row_keys = jax.random.split(key_rows, LAYERS * devices_rv)
    firsts = jax.vmap(lambda one: jax.random.permutation(one, ROW_DEV)[:EXIT_MOST])(row_keys)
    firsts = firsts.reshape(LAYERS, devices_rv, EXIT_MOST).astype(jnp.int32)
    position = jnp.arange(EXIT_MOST, dtype=jnp.int32)[None, None, :]
    slots = jnp.where(position < counts[:, :, None], firsts, ROW_DEV).astype(jnp.int32)
    return slots


def draw_exit_slots(key, part):
    slots = exit_plan(key)
    return slots.reshape(LAYERS, SLOTS)


def draw_hidden(key, part):
    key = jax.random.fold_in(key, 5)
    key_base, key_scale = jax.random.split(key, 2)
    row_scale = jnp.exp(jax.random.uniform(key_scale, (LAYERS, ROWS, 1), jnp.float32, jnp.log(0.03), jnp.log(0.3)))
    base = jnp.clip(jax.random.normal(key_base, (LAYERS, ROWS, D), jnp.float32), -6.0, 6.0)
    values = base * row_scale
    return values.astype(jnp.bfloat16)


def draw_head(key, part):
    key = jax.random.fold_in(key, 7)
    key_base = jax.random.fold_in(key, 0)
    values = jnp.clip(jax.random.normal(key_base, (D, VOCAB), jnp.float32), -6.0, 6.0) * 3.0 / D ** 0.5
    return values.astype(jnp.bfloat16)


def with_ends(values, stream_key, least, largest):
    dims = values.shape
    place = [jax.random.randint(jax.random.fold_in(stream_key, axis), (), 0, dims[axis]) for axis in range(len(dims))]
    values = values.at[tuple(place)].set(least)
    longest = dims.index(max(dims))
    place[longest] = (place[longest] + 1) % dims[longest]
    return values.at[tuple(place)].set(largest)


def rank_bounds(number_of, lean):
    weights = [(1 << 20) // math.isqrt(grade ** lean) + 1 for grade in range(1, number_of + 1)]
    scale = 1 + sum(weights) // (1 << 30)
    return np.cumsum(np.array([max(1, weight // scale) for weight in weights]))


def ranked(own_key, dims, amount, lean):
    grid = rank_bounds(amount, lean)
    lot = jax.random.randint(jax.random.fold_in(own_key, 1), dims, 0, int(grid[amount - 1]))
    standing = jnp.searchsorted(jnp.asarray(grid, jnp.int32), lot, side="right")
    return jax.random.permutation(jax.random.fold_in(own_key, 2), amount)[standing].astype(jnp.int32)


def setup_inputs(seed: int = 0) -> dict:
    key_list = jax.random.split(jax.random.key(seed), 6)
    return {
        "hidden": draw_hidden(jax.random.fold_in(key_list[5], 71), 0),
        "gain": jnp.clip(1.0 + 0.1 * jax.random.normal(key_list[1], (D,), jnp.float32), 0.5, 1.5).astype(jnp.bfloat16),
        "head": draw_head(jax.random.fold_in(key_list[5], 71), 0),
        "exit_slots": draw_exit_slots(jax.random.fold_in(key_list[5], 71), 0),
        "targets": with_ends(ranked(key_list[4], (ROWS,), VOCAB, 2), jax.random.fold_in(key_list[4], 3), 0, VOCAB - 1).astype(jnp.int32),
    }


EPS = 1e-05

def reference(hidden, gain, head, exit_slots, targets):
    devices_rv = N_ROWS * N_VOCAB
    slots = exit_slots.reshape(LAYERS, devices_rv, EXIT_MOST)
    flags_all = slots < ROW_DEV
    offsets = (jnp.arange(devices_rv, dtype=jnp.int32) * ROW_DEV)[None, :, None]
    rows_index = (offsets + jnp.minimum(slots, ROW_DEV - 1)).astype(jnp.int32).reshape(LAYERS, SLOTS)
    flags_all = flags_all.reshape(LAYERS, SLOTS)
    gain_f = gain.astype(jnp.float32)
    columns = jnp.arange(VOCAB, dtype=jnp.int32)

    def one_layer(layer_in):
        layer_rows, index, flags = layer_in
        values = jnp.where(flags[:, None], layer_rows[index], jnp.zeros((), jnp.bfloat16)).astype(jnp.float32)
        labels = jnp.where(flags, targets[index], -1).astype(jnp.int32)
        weight = flags.astype(jnp.float32)
        scale = lax.rsqrt(lax.optimization_barrier(jnp.mean(values * values, axis=1)) + EPS)
        normed = (values * scale[:, None] * gain_f).astype(jnp.bfloat16)
        logits = jnp.dot(normed, head, preferred_element_type=jnp.float32)
        peak = lax.optimization_barrier(jnp.max(logits, axis=1))
        shifted = jnp.exp(logits - peak[:, None])
        mass = lax.optimization_barrier(jnp.sum(shifted, axis=1))
        hits = columns[None, :] == labels[:, None]
        aimed = lax.optimization_barrier(jnp.sum(jnp.where(hits, logits, jnp.zeros((), jnp.float32)), axis=1))
        loss_rows = (peak + jnp.log(mass) - aimed) * weight
        slope = ((shifted / mass[:, None] - hits.astype(jnp.float32)) * weight[:, None]).astype(jnp.bfloat16)
        back = jnp.dot(slope, head.T, preferred_element_type=jnp.float32)
        dots = lax.optimization_barrier(jnp.sum(values * gain_f * back, axis=1))
        grads = scale[:, None] * gain_f * back - values * (scale ** 3)[:, None] * dots[:, None] / D
        return (loss_rows, grads.astype(jnp.bfloat16))
    loss_rows, exit_grads = lax.map(one_layer, (hidden, rows_index, flags_all))
    loss_sum = lax.optimization_barrier(jnp.sum(loss_rows.reshape(LAYERS, N_ROWS, N_VOCAB * EXIT_MOST), axis=2))
    live_sum = lax.optimization_barrier(jnp.sum(flags_all.astype(jnp.float32).reshape(LAYERS, N_ROWS, N_VOCAB * EXIT_MOST), axis=2))
    return (exit_grads, loss_sum / live_sum)
```

```python
import functools

import jax
import jax.numpy as jnp
from jax import lax
from jax.experimental import pallas as pl
from jax.experimental.pallas import tpu as pltpu
from jax.sharding import Mesh, PartitionSpec as P

EPS = 1e-05
LIVE = 72
F32 = jnp.float32
BF16 = jnp.bfloat16


def params():
    return pltpu.CompilerParams(vmem_limit_bytes=40 * 1024 * 1024)


def hits_of(label, first, span):
    column = first + lax.broadcasted_iota(jnp.int32, (span, LIVE), 0)
    return column == label


def logits_kernel(first_ref, normed_ref, head_ref, label_ref, logits_ref, stats_ref):
    step = pl.program_id(0)
    part = lax.dot_general(
        head_ref[0], normed_ref[0], (((1,), (1,)), ((), ())), preferred_element_type=F32
    )

    @pl.when(step == 0)
    def _():
        logits_ref[...] = part

    @pl.when(step > 0)
    def _():
        logits_ref[...] += part

    @pl.when(step == pl.num_programs(0) - 1)
    def _():
        logits = logits_ref[...]
        hits = hits_of(label_ref[...], first_ref[0], logits.shape[0])
        peak = jnp.max(logits, axis=0, keepdims=True)
        shifted = jnp.exp(logits - peak)
        stats_ref[0:1, :] = peak
        stats_ref[1:2, :] = jnp.sum(shifted, axis=0, keepdims=True)
        stats_ref[2:3, :] = jnp.sum(shifted * logits, axis=0, keepdims=True)
        stats_ref[3:4, :] = jnp.sum(jnp.where(hits, logits, 0.0), axis=0, keepdims=True)


def local_logits(first, normed, head, label):
    parts, span, width = head.shape
    return pl.pallas_call(
        logits_kernel,
        grid=(parts,),
        in_specs=[
            pl.BlockSpec(memory_space=pltpu.SMEM),
            pl.BlockSpec((1, LIVE, width), lambda i: (i // 2, 0, i % 2)),
            pl.BlockSpec((1, span, width), lambda i: (i, 0, 0)),
            pl.BlockSpec((1, LIVE), lambda i: (0, 0)),
        ],
        out_specs=[
            pl.BlockSpec((span, LIVE), lambda i: (0, 0)),
            pl.BlockSpec((4, LIVE), lambda i: (0, 0)),
        ],
        out_shape=[
            jax.ShapeDtypeStruct((span, LIVE), F32),
            jax.ShapeDtypeStruct((4, LIVE), F32),
        ],
        compiler_params=params(),
        name="logits",
    )(first, normed, head, label)


def back_kernel(
    first_ref, core_ref, stats_ref, logits_ref, head_ref, label_ref, layer_ref,
    keep_ref, send_ref, row_ref, loss_ref, slope_ref,
):
    step = pl.program_id(0)

    @pl.when(step == 0)
    def _():
        stats = stats_ref[...]
        peaks = [stats[:, 4 * c, :] for c in range(2)]
        peak = jnp.max(jnp.maximum(peaks[0], peaks[1]), axis=0, keepdims=True)
        weight = [jnp.exp(p - peak) for p in peaks]
        mass = sum(weight[c] * stats[:, 4 * c + 1, :] for c in range(2))
        mass = jnp.sum(mass, axis=0, keepdims=True)
        mean = sum(weight[c] * stats[:, 4 * c + 2, :] for c in range(2))
        mean = jnp.sum(mean, axis=0, keepdims=True) / mass
        aimed = jnp.sum(stats[:, 3, :] + stats[:, 7, :], axis=0, keepdims=True)
        row_ref[...] = mean - aimed
        loss = peak + jnp.log(mass) - aimed
        for layer in range(2):
            mine = (layer_ref[...] == layer).astype(F32)
            total = jnp.sum(loss * mine, axis=1, keepdims=True)
            loss_ref[layer : layer + 1, :] = total / jnp.sum(mine, axis=1, keepdims=True)
        logits = logits_ref[...]
        hits = hits_of(label_ref[...], first_ref[0], logits.shape[0])
        slope = jnp.exp(logits - peak) / mass - hits.astype(F32)
        slope_ref[...] = slope.T.astype(BF16)

    part = jnp.dot(slope_ref[...], head_ref[0], preferred_element_type=F32)

    @pl.when(step % 2 == core_ref[0])
    def _():
        keep_ref[step // 2] = part

    @pl.when(step % 2 != core_ref[0])
    def _():
        send_ref[step // 2] = part


def local_back(first, core, stats, logits, head, label, layer):
    parts, span, width = head.shape
    whole = lambda shape: pl.BlockSpec(shape, lambda i: (0,) * len(shape))
    half = (parts // 2, LIVE, width)
    return pl.pallas_call(
        back_kernel,
        grid=(parts,),
        in_specs=[
            pl.BlockSpec(memory_space=pltpu.SMEM),
            pl.BlockSpec(memory_space=pltpu.SMEM),
            whole(stats.shape),
            whole(logits.shape),
            pl.BlockSpec((1, span, width), lambda i: (i, 0, 0)),
            whole((1, LIVE)),
            whole((1, LIVE)),
        ],
        out_specs=[whole(half), whole(half), whole((1, LIVE)), whole((2, 1))],
        out_shape=[
            jax.ShapeDtypeStruct(half, F32),
            jax.ShapeDtypeStruct(half, F32),
            jax.ShapeDtypeStruct((1, LIVE), F32),
            jax.ShapeDtypeStruct((2, 1), F32),
        ],
        scratch_shapes=[pltpu.VMEM((LIVE, span), BF16)],
        compiler_params=params(),
        name="back",
    )(first, core, stats, logits, head, label, layer)


def spread(values, axes, count):
    copies = jnp.broadcast_to(values[None], (count, *values.shape))
    return lax.all_to_all(copies, axes, 0, 0, tiled=True)


def swap_core(values):
    return lax.ppermute(values, "c", [(0, 1), (1, 0)])


def body(hidden, gain, head, exit_slots, targets):
    layers, row_dev, part_width = hidden.shape
    most = exit_slots.shape[1]
    own = layers * most
    width = gain.shape[0]
    span = head.shape[1]
    y, c, x = (lax.axis_index(name) for name in ("y", "c", "x"))
    first = (((y * 2 + c) * 4 + x) * span).astype(jnp.int32).reshape(1)
    core = c.astype(jnp.int32).reshape(1)

    full_head = lax.all_gather(head.T, "z", axis=0)

    live = exit_slots < row_dev
    local = jnp.minimum(exit_slots, row_dev - 1)
    picked = jax.vmap(lambda block, index: block[index])(hidden, local)
    picked = jnp.where(live[:, :, None], picked, jnp.zeros_like(picked))
    label = jnp.where(live, targets[local], 0)
    layer = jnp.broadcast_to(jnp.arange(layers)[:, None], live.shape)
    facts = jnp.stack([live.astype(jnp.int32), label // 256, label % 256, layer], axis=2)
    facts = jnp.pad(facts.astype(BF16), ((0, 0), (0, 0), (0, 124)))
    packed = jnp.concatenate([picked, facts], axis=2).reshape(own, part_width + 128)
    pair = lax.all_gather(packed, "c", axis=0, tiled=True)
    slots = spread(pair, "y", 8).reshape(16 * own, part_width + 128)

    total = slots.shape[0]
    flag = slots[:, part_width].astype(F32)
    below = (jnp.arange(total)[:, None] < jnp.arange(total)[None, :]).astype(F32)
    rank = jnp.sum(below * flag[:, None], axis=0)
    place = (rank[None, :] == jnp.arange(LIVE, dtype=F32)[:, None]) & (flag > 0)[None, :]
    place = place.astype(BF16)
    compact = jnp.dot(place, slots, preferred_element_type=F32)
    fact = compact[:, part_width : part_width + 4].astype(jnp.int32).T
    label_row = (fact[1] * 256 + fact[2]).reshape(1, LIVE)
    layer_row = fact[3].reshape(1, LIVE)
    rows = spread(compact[:, :part_width].astype(BF16), "x", 4)

    values = rows.astype(F32)
    scale = lax.rsqrt(jnp.sum(values * values, axis=(0, 2)) / width + EPS)
    gain_f = gain.astype(F32)
    normed = values * scale[None, :, None] * gain_f.reshape(4, 1, part_width)
    normed = normed.astype(BF16)

    logits, stats = local_logits(first, normed, full_head, label_row)
    stats = lax.all_gather(stats, "c", axis=0, tiled=True)
    stats = spread(stats, ("y", "x"), 32)
    keep, send, gap, group_loss = local_back(
        first, core, stats, logits, full_head, label_row, layer_row
    )
    part = (keep + swap_core(send)).astype(BF16)
    part = lax.all_to_all(part, "x", 0, 0, tiled=True)
    part = jnp.sum(part.astype(F32), axis=0).astype(BF16)
    sent = lax.dot_general(place, part, (((0,), (0,)), ((), ())), preferred_element_type=F32)
    sent = sent.astype(BF16).reshape(8, 2 * own, part_width // 2)
    back = jnp.sum(lax.all_to_all(sent, "y", 0, 0, tiled=True).astype(F32), axis=0)

    half = part_width // 2
    start = x * part_width + c * half
    gain_half = lax.dynamic_slice_in_dim(gain_f, start, half)
    value_half = lax.dynamic_slice_in_dim(pair, c * half, half, 1).astype(F32)
    mine = lax.dynamic_slice_in_dim(place, y * 2 * own, 2 * own, 1).astype(F32)
    scale_own = jnp.sum(mine * scale[:, None], axis=0)
    shift_own = jnp.sum(mine * (scale**3 * gap[0] / scale / width)[:, None], axis=0)
    grads = scale_own[:, None] * gain_half * back - value_half * shift_own[:, None]
    grads = grads.astype(BF16).reshape(2, own, half)
    kept = lax.dynamic_index_in_dim(grads, c, 0, keepdims=False)
    came = swap_core(lax.dynamic_index_in_dim(grads, 1 - c, 0, keepdims=False))
    low = jnp.where(c == 0, kept, came)
    high = jnp.where(c == 0, came, kept)
    exit_grads = jnp.concatenate([low, high], axis=1).reshape(layers, most, part_width)
    return exit_grads, group_loss


def solution(mesh):
    split = Mesh(mesh.devices.reshape(8, 8, 2, 4), ("z", "y", "c", "x"))
    in_specs = (
        P(None, ("z", "y", "c"), "x"),
        P(),
        P("z", ("y", "c", "x")),
        P(None, ("z", "y", "c")),
        P(("z", "y", "c")),
    )
    out_specs = (P(None, ("z", "y", "c"), "x"), P(None, "z"))
    return jax.shard_map(body, mesh=split, in_specs=in_specs, out_specs=out_specs, check_vma=False)
```

```python
import functools

import jax
import jax.numpy as jnp
from jax import lax
from jax.experimental import pallas as pl
from jax.experimental.pallas import tpu as pltpu
from jax.sharding import Mesh, PartitionSpec as P

EPS = 1e-05
LIVE = 72
SPAN = 500
PART = 256
EARLY = 5
WIDTH = 640
F32 = jnp.float32
BF16 = jnp.bfloat16


def params():
    return pltpu.CompilerParams(vmem_limit_bytes=56 * 1024 * 1024)


def fetch(refs, buffers, sem):
    copies = [pltpu.make_async_copy(ref, buf, sem.at[i]) for i, (ref, buf) in enumerate(zip(refs, buffers))]
    for copy in copies:
        copy.start()
    return copies


def scores(shard, normed_ref, head):
    normed = normed_ref[lax.rem(shard, 2), shard // 2]
    return lax.dot_general(head, normed, (((1,), (1,)), ((), ())), preferred_element_type=F32)


def first_kernel(meta_ref, normed_ref, *rest):
    refs, (logits_ref, full, sem) = rest[:EARLY], rest[EARLY:]
    copies = fetch(refs, [full.at[i] for i in range(EARLY)], sem)
    total = jnp.zeros((SPAN, LIVE), F32)
    for place, copy in enumerate(copies):
        copy.wait()
        total += scores(meta_ref[2 + place], normed_ref, full[place])
    logits_ref[...] = total


def logits_kernel(meta_ref, normed_ref, label_ref, first_ref, *rest):
    refs, (logits_ref, stats_ref, full, low, high, sem) = rest[: 9 - EARLY], rest[9 - EARLY :]
    count = 7 - EARLY
    copies = fetch(refs, [*(full.at[i] for i in range(count)), low, high], sem)
    total = first_ref[...]
    for i in range(count):
        copies[i].wait()
        total += scores(meta_ref[2 + EARLY + i], normed_ref, full[i])
    copies[count].wait()
    part = scores(meta_ref[9], normed_ref, low[...])
    copies[count + 1].wait()
    logits = total + jnp.concatenate([part, scores(meta_ref[9], normed_ref, high[...])], axis=0)
    logits_ref[...] = logits
    column = lax.broadcasted_iota(jnp.int32, (SPAN, LIVE), 0)
    hits = column + meta_ref[0] == label_ref[...]
    peak = jnp.max(logits, axis=0, keepdims=True)
    shifted = jnp.exp(logits - peak)
    stats_ref[0:1, :] = peak
    stats_ref[1:2, :] = jnp.sum(shifted, axis=0, keepdims=True)
    stats_ref[2:3, :] = jnp.sum(shifted * (logits - peak), axis=0, keepdims=True)
    stats_ref[3:4, :] = jnp.sum(jnp.where(hits, logits, 0.0), axis=0, keepdims=True)


VMEM = pl.BlockSpec(memory_space=pltpu.VMEM)
SMEM = pl.BlockSpec(memory_space=pltpu.SMEM)
ANY = pl.BlockSpec(memory_space=pl.ANY)


def head_scratch(full, halves):
    buffers = [pltpu.VMEM((full, SPAN, WIDTH), BF16)]
    if halves:
        buffers += [pltpu.VMEM((rows, WIDTH), BF16) for rows in (PART, SPAN - PART)]
    return [*buffers, pltpu.SemaphoreType.DMA((full + 2 * halves,))]


def local_logits(meta, normed, label, near):
    first = pl.pallas_call(
        first_kernel,
        in_specs=[SMEM, VMEM, *[ANY] * EARLY],
        out_specs=VMEM,
        out_shape=jax.ShapeDtypeStruct((SPAN, LIVE), F32),
        scratch_shapes=head_scratch(EARLY, 0),
        compiler_params=params(),
        cost_estimate=pl.CostEstimate(
            flops=2 * EARLY * SPAN * LIVE * WIDTH,
            bytes_accessed=2 * EARLY * SPAN * WIDTH,
            transcendentals=0,
        ),
        name="logits_early",
    )(meta, normed, *near[:EARLY])
    return pl.pallas_call(
        logits_kernel,
        in_specs=[SMEM, VMEM, VMEM, VMEM, *[ANY] * (9 - EARLY)],
        out_specs=[VMEM, VMEM],
        out_shape=[
            jax.ShapeDtypeStruct((SPAN, LIVE), F32),
            jax.ShapeDtypeStruct((4, LIVE), F32),
        ],
        scratch_shapes=head_scratch(7 - EARLY, 1),
        compiler_params=params(),
        name="logits",
    )(meta, normed, label, first, *near[EARLY:])


def back_kernel(meta_ref, stats_ref, logits_ref, label_ref, layer_ref, *rest):
    refs, (keep_ref, send_ref, row_ref, loss_ref, full, low, high, sem) = rest[:9], rest[9:]
    copies = fetch(refs, [*(full.at[i] for i in range(7)), low, high], sem)
    stats = stats_ref[...]
    peaks = [stats[:, 4 * c, :] for c in range(2)]
    peak = jnp.max(jnp.maximum(peaks[0], peaks[1]), axis=0, keepdims=True)
    mass = mean = aimed = jnp.zeros((1, LIVE), F32)
    for c in range(2):
        weight = jnp.exp(peaks[c] - peak)
        own = stats[:, 4 * c + 1, :]
        mass += jnp.sum(weight * own, axis=0, keepdims=True)
        moved = stats[:, 4 * c + 2, :] + (peaks[c] - peak) * own
        mean += jnp.sum(weight * moved, axis=0, keepdims=True)
        aimed += jnp.sum(stats[:, 4 * c + 3, :], axis=0, keepdims=True)
    row_ref[...] = mean / mass + (peak - aimed)
    loss = jnp.log(mass) + (peak - aimed)
    for layer in range(2):
        mine = (layer_ref[...] == layer).astype(F32)
        total = jnp.sum(loss * mine, axis=1, keepdims=True)
        loss_ref[layer : layer + 1, :] = total / jnp.sum(mine, axis=1, keepdims=True)
    logits = logits_ref[...]
    column = lax.broadcasted_iota(jnp.int32, (SPAN, LIVE), 0)
    hits = (column + meta_ref[0] == label_ref[...]).astype(F32)
    slope = (jnp.exp(logits - peak) / mass - hits).T.astype(BF16)
    for place in range(8):
        shard = meta_ref[2 + place]
        copies[place].wait()
        if place < 7:
            part = jnp.dot(slope, full[place], preferred_element_type=F32)
        else:
            copies[8].wait()
            part = jnp.dot(slope[:, :PART], low[...], preferred_element_type=F32)
            part += jnp.dot(slope[:, PART:], high[...], preferred_element_type=F32)
        kept = lax.rem(shard, 2) == meta_ref[1]

        @pl.when(kept)
        def _():
            keep_ref[shard // 2] = part

        @pl.when(jnp.logical_not(kept))
        def _():
            send_ref[shard // 2] = part


def local_back(meta, stats, logits, label, layer, near):
    half = (4, LIVE, WIDTH)
    return pl.pallas_call(
        back_kernel,
        in_specs=[SMEM, VMEM, VMEM, VMEM, VMEM, *[ANY] * 9],
        out_specs=[VMEM] * 4,
        out_shape=[
            jax.ShapeDtypeStruct(half, F32),
            jax.ShapeDtypeStruct(half, F32),
            jax.ShapeDtypeStruct((1, LIVE), F32),
            jax.ShapeDtypeStruct((2, 1), F32),
        ],
        scratch_shapes=head_scratch(7, 1),
        compiler_params=params(),
        name="back",
    )(meta, stats, logits, label, layer, *near)


def spread(values, axes, count):
    copies = jnp.broadcast_to(values[None], (count, *values.shape))
    return lax.all_to_all(copies, axes, 0, 0, tiled=True)


def swap_core(values):
    return lax.ppermute(values, "c", [(0, 1), (1, 0)])


def ring(own):
    up = [(i, (i + 1) % 8) for i in range(8)]
    down = [(i, (i - 1) % 8) for i in range(8)]
    right = left = own
    near = [own]
    for _ in range(3):
        right = lax.ppermute(right, "z", up)
        left = lax.ppermute(left, "z", down)
        near += [right, left]
    near.append(lax.ppermute(right[:PART], "z", up))
    near.append(lax.ppermute(left[PART:], "z", down))
    return near


def body(hidden, gain, head, exit_slots, targets):
    layers, row_dev, part_width = hidden.shape
    most = exit_slots.shape[1]
    own = layers * most
    width = gain.shape[0]
    half = part_width // 2
    z, y, c, x = (lax.axis_index(name) for name in ("z", "y", "c", "x"))
    shards = [lax.rem(z + s, 8) for s in (0, 7, 1, 6, 2, 5, 3, 4)]
    first = ((y * 2 + c) * 4 + x) * SPAN
    meta = jnp.stack([first, c, *shards]).astype(jnp.int32)
    near = ring(head.T)

    live = exit_slots < row_dev
    local = jnp.minimum(exit_slots, row_dev - 1)
    picked = jax.vmap(lambda block, index: block[index])(hidden, local)
    picked = jnp.where(live[:, :, None], picked, jnp.zeros_like(picked))
    label = jnp.where(live, targets[local], 0)
    layer = jnp.broadcast_to(jnp.arange(layers)[:, None], live.shape)
    facts = jnp.stack([live.astype(jnp.int32), label // 256, label % 256, layer], axis=2)
    facts = jnp.pad(facts.astype(BF16), ((0, 0), (0, 0), (0, 124)))
    packed = jnp.concatenate([picked, facts], axis=2).reshape(own, part_width + 128)
    pair = lax.all_gather(packed, "c", axis=0, tiled=True)
    pair_half = lax.dynamic_slice_in_dim(pair, c * half, half, 1)
    slots = jnp.concatenate([pair_half, pair[:, part_width:]], axis=1)
    slots = spread(slots, "y", 8).reshape(16 * own, half + 128)

    total = slots.shape[0]
    flag = slots[:, half].astype(F32)
    below = (jnp.arange(total)[:, None] < jnp.arange(total)[None, :]).astype(F32)
    rank = jnp.sum(below * flag[:, None], axis=0)
    place = (rank[None, :] == jnp.arange(LIVE, dtype=F32)[:, None]) & (flag > 0)[None, :]
    place = place.astype(BF16)
    compact = jnp.dot(place, slots, preferred_element_type=F32)
    fact = compact[:, half : half + 4].astype(jnp.int32).T
    label_row = (fact[1] * 256 + fact[2]).reshape(1, LIVE)
    layer_row = fact[3].reshape(1, LIVE)
    rows = spread(compact[:, :half].astype(BF16), "x", 4)
    rows = lax.all_gather(rows, "c", axis=0)

    values = rows.astype(F32)
    scale = lax.rsqrt(jnp.sum(values * values, axis=(0, 1, 3)) / width + EPS)
    gain_f = gain.astype(F32)
    gain_rows = gain_f.reshape(4, 2, 1, half).transpose(1, 0, 2, 3)
    normed = (values * scale[:, None] * gain_rows).astype(BF16)

    logits, stats = local_logits(meta, normed, label_row, near)
    stats = lax.all_gather(stats, "c", axis=0, tiled=True)
    stats = spread(stats, ("y", "x"), 32)
    keep, send, gap, group_loss = local_back(
        meta, stats, logits, label_row, layer_row, near
    )
    part = (keep + swap_core(send)).astype(BF16)
    part = lax.all_to_all(part, "x", 0, 0, tiled=True)
    part = jnp.sum(part.astype(F32), axis=0).astype(BF16)
    sent = lax.dot_general(place, part, (((0,), (0,)), ((), ())), preferred_element_type=F32)
    sent = sent.astype(BF16).reshape(8, 2 * own, half)
    back = jnp.sum(lax.all_to_all(sent, "y", 0, 0, tiled=True).astype(F32), axis=0)

    start = x * part_width + c * half
    gain_half = lax.dynamic_slice_in_dim(gain_f, start, half)
    value_half = pair_half.astype(F32)
    mine = lax.dynamic_slice_in_dim(place, y * 2 * own, 2 * own, 1).astype(F32)
    scale_own = jnp.sum(mine * scale[:, None], axis=0)
    shift_own = jnp.sum(mine * (scale**2 * gap[0] / width)[:, None], axis=0)
    grads = scale_own[:, None] * gain_half * back - value_half * shift_own[:, None]
    grads = grads.astype(BF16).reshape(2, own, half)
    kept = lax.dynamic_index_in_dim(grads, c, 0, keepdims=False)
    came = swap_core(lax.dynamic_index_in_dim(grads, 1 - c, 0, keepdims=False))
    low = jnp.where(c == 0, kept, came)
    high = jnp.where(c == 0, came, kept)
    exit_grads = jnp.concatenate([low, high], axis=1).reshape(layers, most, part_width)
    return exit_grads, group_loss


def solution(mesh):
    split = Mesh(mesh.devices.reshape(8, 8, 2, 4), ("z", "y", "c", "x"))
    in_specs = (
        P(None, ("z", "y", "c"), "x"),
        P(),
        P("z", ("y", "c", "x")),
        P(None, ("z", "y", "c")),
        P(("z", "y", "c")),
    )
    out_specs = (P(None, ("z", "y", "c"), "x"), P(None, "z"))
    return jax.shard_map(body, mesh=split, in_specs=in_specs, out_specs=out_specs, check_vma=False)
```

```python
import functools

import jax
import jax.numpy as jnp
from jax import lax
from jax.experimental import pallas as pl
from jax.experimental.pallas import tpu as pltpu
from jax.sharding import Mesh, PartitionSpec as P

EPS = 1e-05
LIVE = 72
SPAN = 500
PART = 256
NEAR = 7
WIDTH = 640
FACTS = 128
F32 = jnp.float32
BF16 = jnp.bfloat16


def params():
    return pltpu.CompilerParams(vmem_limit_bytes=32 * 1024 * 1024)


def pick_kernel(slots_ref, targets_ref, hidden_ref, out_ref, rows, total, sem):
    layers, most = slots_ref.shape
    part_width = hidden_ref.shape[2]
    copies = []
    for i in range(layers * most):
        row = jnp.minimum(slots_ref[i // most, i % most], hidden_ref.shape[1] - 1)
        block = pl.ds(pl.multiple_of((row // 16) * 16, 16), 16)
        copies.append(pltpu.make_async_copy(hidden_ref.at[i // most, block], rows.at[i], sem.at[i]))
        copies[-1].start()
    lane = lax.broadcasted_iota(jnp.int32, (1, FACTS), 1)
    sub = lax.broadcasted_iota(jnp.int32, (16, 1), 0)
    for i, copy in enumerate(copies):
        entry = slots_ref[i // most, i % most]
        row = jnp.minimum(entry, hidden_ref.shape[1] - 1)
        live = (entry < hidden_ref.shape[1]).astype(jnp.int32)
        label = targets_ref[row] * live
        fact = jnp.where(lane == 0, live, 0) + jnp.where(lane == 1, label // 256, 0)
        fact += jnp.where(lane == 2, label % 256, 0) + jnp.where(lane == 3, i // most, 0)
        total[i : i + 1, part_width:] = fact.astype(F32)
        copy.wait()
        mine = (sub == row % 16) & (live > 0)
        picked = jnp.sum(jnp.where(mine, rows[i].astype(F32), 0.0), axis=0, keepdims=True)
        total[i : i + 1, :part_width] = picked
    out_ref[...] = total[...].astype(BF16)


def pick(slots, targets, hidden):
    own, part_width = slots.size, hidden.shape[2]
    return pl.pallas_call(
        pick_kernel,
        in_specs=[SMEM, SMEM, pl.BlockSpec(memory_space=pltpu.HBM)],
        out_specs=VMEM,
        out_shape=jax.ShapeDtypeStruct((own, part_width + FACTS), BF16),
        scratch_shapes=[
            pltpu.VMEM((own, 16, part_width), BF16),
            pltpu.VMEM((own, part_width + FACTS), F32),
            pltpu.SemaphoreType.DMA((own,)),
        ],
        compiler_params=params(),
        name="pick",
    )(slots, targets, hidden)


def scores(shard, normed_ref, head):
    normed = normed_ref[lax.rem(shard, 2), shard // 2]
    return lax.dot_general(head, normed, (((1,), (1,)), ((), ())), preferred_element_type=F32)


def first_kernel(meta_ref, normed_ref, *rest):
    *refs, logits_ref = rest
    total = jnp.zeros((SPAN, LIVE), F32)
    for place, ref in enumerate(refs):
        total += scores(meta_ref[2 + place], normed_ref, ref[...])
    logits_ref[...] = total


def logits_kernel(meta_ref, normed_ref, label_ref, first_ref, *rest):
    *refs, logits_ref, stats_ref = rest
    parts = [scores(meta_ref[9], normed_ref, ref[...]) for ref in refs]
    logits = first_ref[...] + jnp.concatenate(parts, axis=0)
    logits_ref[...] = logits
    column = lax.broadcasted_iota(jnp.int32, (SPAN, LIVE), 0)
    hits = column + meta_ref[0] == label_ref[...]
    peak = jnp.max(logits, axis=0, keepdims=True)
    shifted = jnp.exp(logits - peak)
    stats_ref[0:1, :] = peak
    stats_ref[1:2, :] = jnp.sum(shifted, axis=0, keepdims=True)
    stats_ref[2:3, :] = jnp.sum(shifted * (logits - peak), axis=0, keepdims=True)
    stats_ref[3:4, :] = jnp.sum(jnp.where(hits, logits, 0.0), axis=0, keepdims=True)


VMEM = pl.BlockSpec(memory_space=pltpu.VMEM)
SMEM = pl.BlockSpec(memory_space=pltpu.SMEM)


def local_logits(meta, normed, label, near):
    first = pl.pallas_call(
        first_kernel,
        in_specs=[SMEM, VMEM, *[VMEM] * NEAR],
        out_specs=VMEM,
        out_shape=jax.ShapeDtypeStruct((SPAN, LIVE), F32),
        compiler_params=params(),
        cost_estimate=pl.CostEstimate(
            flops=2 * NEAR * SPAN * LIVE * WIDTH,
            bytes_accessed=2 * NEAR * SPAN * WIDTH,
            transcendentals=0,
        ),
        name="logits_early",
    )(meta, normed, *near[:NEAR])
    return pl.pallas_call(
        logits_kernel,
        in_specs=[SMEM, VMEM, VMEM, VMEM, *[VMEM] * (9 - NEAR)],
        out_specs=[VMEM, VMEM],
        out_shape=[
            jax.ShapeDtypeStruct((SPAN, LIVE), F32),
            jax.ShapeDtypeStruct((4, LIVE), F32),
        ],
        compiler_params=params(),
        name="logits",
    )(meta, normed, label, first, *near[NEAR:])


def back_kernel(meta_ref, stats_ref, logits_ref, label_ref, layer_ref, *rest):
    *refs, part_ref, row_ref, loss_ref = rest
    stats = stats_ref[...]
    peaks = [stats[:, 4 * c, :] for c in range(2)]
    peak = jnp.max(jnp.maximum(peaks[0], peaks[1]), axis=0, keepdims=True)
    mass = mean = aimed = jnp.zeros((1, LIVE), F32)
    for c in range(2):
        weight = jnp.exp(peaks[c] - peak)
        own = stats[:, 4 * c + 1, :]
        mass += jnp.sum(weight * own, axis=0, keepdims=True)
        moved = stats[:, 4 * c + 2, :] + (peaks[c] - peak) * own
        mean += jnp.sum(weight * moved, axis=0, keepdims=True)
        aimed += jnp.sum(stats[:, 4 * c + 3, :], axis=0, keepdims=True)
    row_ref[...] = mean / mass + (peak - aimed)
    loss = jnp.log(mass) + (peak - aimed)
    for layer in range(2):
        mine = (layer_ref[...] == layer).astype(F32)
        total = jnp.sum(loss * mine, axis=1, keepdims=True)
        loss_ref[layer : layer + 1, :] = total / jnp.sum(mine, axis=1, keepdims=True)
    logits = logits_ref[...]
    column = lax.broadcasted_iota(jnp.int32, (SPAN, LIVE), 0)
    hits = (column + meta_ref[0] == label_ref[...]).astype(F32)
    slope = (jnp.exp(logits - peak) / mass - hits).T.astype(BF16)
    for place in range(8):
        shard = meta_ref[2 + place]
        if place < 7:
            part = jnp.dot(slope, refs[place][...], preferred_element_type=F32)
        else:
            part = jnp.dot(slope[:, :PART], refs[7][...], preferred_element_type=F32)
            part += jnp.dot(slope[:, PART:], refs[8][...], preferred_element_type=F32)
        part_ref[shard] = part.astype(BF16)


def local_back(meta, stats, logits, label, layer, near):
    return pl.pallas_call(
        back_kernel,
        in_specs=[SMEM, VMEM, VMEM, VMEM, VMEM, *[VMEM] * 9],
        out_specs=[VMEM] * 3,
        out_shape=[
            jax.ShapeDtypeStruct((8, LIVE, WIDTH), BF16),
            jax.ShapeDtypeStruct((1, LIVE), F32),
            jax.ShapeDtypeStruct((2, 1), F32),
        ],
        compiler_params=params(),
        name="back",
    )(meta, stats, logits, label, layer, *near)


def spread(values, axes, count):
    copies = jnp.broadcast_to(values[None], (count, *values.shape))
    return lax.all_to_all(copies, axes, 0, 0, tiled=True)


def ring(own):
    up = [(i, (i + 1) % 8) for i in range(8)]
    down = [(i, (i - 1) % 8) for i in range(8)]
    right = left = own
    near = [own]
    for _ in range(3):
        right = lax.ppermute(right, "z", up)
        left = lax.ppermute(left, "z", down)
        near += [right, left]
    near.append(lax.ppermute(right[:PART], "z", up))
    near.append(lax.ppermute(left[PART:], "z", down))
    return near


def body(hidden, gain, head, exit_slots, targets):
    layers, row_dev, part_width = hidden.shape
    most = exit_slots.shape[1]
    own = layers * most
    width = gain.shape[0]
    half = part_width // 2
    z, y, c, x = (lax.axis_index(name) for name in ("z", "y", "c", "x"))
    shards = [lax.rem(z + s, 8) for s in (0, 7, 1, 6, 2, 5, 3, 4)]
    first = ((y * 2 + c) * 4 + x) * SPAN
    meta = jnp.stack([first, c, *shards]).astype(jnp.int32)
    near = ring(head.T)

    packed = pick(exit_slots, targets, hidden)
    picked = packed[:, :part_width]
    pair = lax.all_gather(packed, "c", axis=0, tiled=True)
    pair_half = lax.dynamic_slice_in_dim(pair, c * half, half, 1)
    slots = jnp.concatenate([pair_half, pair[:, part_width:]], axis=1)
    slots = spread(slots, "y", 8).reshape(16 * own, half + 128)

    total = slots.shape[0]
    flag = slots[:, half].astype(F32)
    below = (jnp.arange(total)[:, None] < jnp.arange(total)[None, :]).astype(F32)
    rank = jnp.sum(below * flag[:, None], axis=0)
    place = (rank[None, :] == jnp.arange(LIVE, dtype=F32)[:, None]) & (flag > 0)[None, :]
    place = place.astype(BF16)
    place_out = jnp.pad(place.reshape(LIVE, 16, own), ((0, 0), (0, 0), (0, 16 - own)))
    place_out = place_out.reshape(LIVE, 256)
    compact = jnp.dot(place, slots, preferred_element_type=F32)
    fact = compact[:, half : half + 4].astype(jnp.int32).T
    label_row = (fact[1] * 256 + fact[2]).reshape(1, LIVE)
    layer_row = fact[3].reshape(1, LIVE)
    rows = spread(compact[:, :half].astype(BF16), "x", 4)
    rows = lax.all_gather(rows, "c", axis=0)

    values = rows.astype(F32)
    scale = lax.rsqrt(jnp.sum(values * values, axis=(0, 1, 3)) / width + EPS)
    gain_f = gain.astype(F32)
    gain_rows = gain_f.reshape(4, 2, 1, half).transpose(1, 0, 2, 3)
    normed = (values * scale[:, None] * gain_rows).astype(BF16)

    logits, stats = local_logits(meta, normed, label_row, near)
    stats = lax.all_gather(stats, "c", axis=0, tiled=True)
    stats = spread(stats, ("y", "x"), 32)
    part, gap, group_loss = local_back(meta, stats, logits, label_row, layer_row, near)

    part = lax.all_to_all(part, ("x", "c"), 0, 0, tiled=True)
    part = jnp.sum(part.astype(F32), axis=0).astype(BF16)
    sent = lax.dot_general(place_out, part, (((0,), (0,)), ((), ())), preferred_element_type=F32)
    sent = sent.astype(BF16).reshape(16, 16, half)
    back = lax.all_to_all(sent, ("y", "c"), 0, 0, tiled=True)
    back = jnp.sum(back.reshape(8, 2, 16, half).astype(F32), axis=0)[:, :own]

    gain_own = lax.dynamic_slice_in_dim(gain_f, x * part_width, part_width)
    mine = lax.dynamic_slice_in_dim(place, (y * 2 + c) * own, own, 1).astype(F32)
    scale_own = jnp.sum(mine * scale[:, None], axis=0)
    shift_own = jnp.sum(mine * (scale**2 * gap[0] / width)[:, None], axis=0)
    value_own = picked.reshape(own, 2, half).transpose(1, 0, 2).astype(F32)
    grads = scale_own[:, None] * gain_own.reshape(2, 1, half) * back - value_own * shift_own[:, None]
    exit_grads = grads.astype(BF16).transpose(1, 0, 2).reshape(layers, most, part_width)
    return exit_grads, group_loss


def solution(mesh):
    split = Mesh(mesh.devices.reshape(8, 8, 2, 4), ("z", "y", "c", "x"))
    in_specs = (
        P(None, ("z", "y", "c"), "x"),
        P(),
        P("z", ("y", "c", "x")),
        P(None, ("z", "y", "c")),
        P(("z", "y", "c")),
    )
    out_specs = (P(None, ("z", "y", "c"), "x"), P(None, "z"))
    return jax.shard_map(body, mesh=split, in_specs=in_specs, out_specs=out_specs, check_vma=False)
```

```python
import functools

import jax
import jax.numpy as jnp
from jax import lax
from jax.experimental import pallas as pl
from jax.experimental.pallas import tpu as pltpu
from jax.sharding import Mesh, PartitionSpec as P

EPS = 1e-05
LIVE = 72
SPAN = 500
PART = 264
NEAR = 7
WIDTH = 640
FACTS = 128
F32 = jnp.float32
BF16 = jnp.bfloat16


def params(mib=32):
    return pltpu.CompilerParams(vmem_limit_bytes=mib * 1024 * 1024)


def pick_kernel(slots_ref, targets_ref, hidden_ref, out_ref, rows, total, sem):
    layers, most = slots_ref.shape
    part_width = hidden_ref.shape[2]
    copies = []
    for i in range(layers * most):
        row = jnp.minimum(slots_ref[i // most, i % most], hidden_ref.shape[1] - 1)
        block = pl.ds(pl.multiple_of((row // 16) * 16, 16), 16)
        copies.append(pltpu.make_async_copy(hidden_ref.at[i // most, block], rows.at[i], sem.at[i]))
        copies[-1].start()
    lane = lax.broadcasted_iota(jnp.int32, (1, FACTS), 1)
    sub = lax.broadcasted_iota(jnp.int32, (16, 1), 0)
    for i, copy in enumerate(copies):
        entry = slots_ref[i // most, i % most]
        row = jnp.minimum(entry, hidden_ref.shape[1] - 1)
        live = (entry < hidden_ref.shape[1]).astype(jnp.int32)
        label = targets_ref[row] * live
        fact = jnp.where(lane == 0, live, 0) + jnp.where(lane == 1, label // 256, 0)
        fact += jnp.where(lane == 2, label % 256, 0) + jnp.where(lane == 3, i // most, 0)
        total[i : i + 1, part_width:] = fact.astype(F32)
        copy.wait()
        mine = (sub == row % 16) & (live > 0)
        picked = jnp.sum(jnp.where(mine, rows[i].astype(F32), 0.0), axis=0, keepdims=True)
        total[i : i + 1, :part_width] = picked
    out_ref[...] = total[...].astype(BF16)


def pick(slots, targets, hidden):
    own, part_width = slots.size, hidden.shape[2]
    return pl.pallas_call(
        pick_kernel,
        in_specs=[SMEM, SMEM, pl.BlockSpec(memory_space=pltpu.HBM)],
        out_specs=VMEM,
        out_shape=jax.ShapeDtypeStruct((own, part_width + FACTS), BF16),
        scratch_shapes=[
            pltpu.VMEM((own, 16, part_width), BF16),
            pltpu.VMEM((own, part_width + FACTS), F32),
            pltpu.SemaphoreType.DMA((own,)),
        ],
        compiler_params=params(56),
        name="pick",
    )(slots, targets, hidden)


def scores(shard, normed_ref, head):
    normed = normed_ref[lax.rem(shard, 2), shard // 2]
    return lax.dot_general(head, normed, (((1,), (1,)), ((), ())), preferred_element_type=F32)


def first_kernel(meta_ref, normed_ref, *rest):
    *refs, logits_ref = rest
    total = jnp.zeros((SPAN, LIVE), F32)
    for place, ref in enumerate(refs):
        total += scores(meta_ref[2 + place], normed_ref, ref[...])
    logits_ref[...] = total


def logits_kernel(meta_ref, normed_ref, label_ref, first_ref, *rest):
    *refs, logits_ref, stats_ref = rest
    parts = [scores(meta_ref[9], normed_ref, ref[...]) for ref in refs]
    logits = first_ref[...] + jnp.concatenate(parts, axis=0)
    logits_ref[...] = logits
    column = lax.broadcasted_iota(jnp.int32, (SPAN, LIVE), 0)
    hits = column + meta_ref[0] == label_ref[...]
    peak = jnp.max(logits, axis=0, keepdims=True)
    shifted = jnp.exp(logits - peak)
    stats_ref[0:1, :] = peak
    stats_ref[1:2, :] = jnp.sum(shifted, axis=0, keepdims=True)
    stats_ref[2:3, :] = jnp.sum(shifted * (logits - peak), axis=0, keepdims=True)
    stats_ref[3:4, :] = jnp.sum(jnp.where(hits, logits, 0.0), axis=0, keepdims=True)


VMEM = pl.BlockSpec(memory_space=pltpu.VMEM)
SMEM = pl.BlockSpec(memory_space=pltpu.SMEM)


def local_logits(meta, normed, label, near):
    first = pl.pallas_call(
        first_kernel,
        in_specs=[SMEM, VMEM, *[VMEM] * NEAR],
        out_specs=VMEM,
        out_shape=jax.ShapeDtypeStruct((SPAN, LIVE), F32),
        compiler_params=params(),
        cost_estimate=pl.CostEstimate(
            flops=2 * NEAR * SPAN * LIVE * WIDTH,
            bytes_accessed=2 * NEAR * SPAN * WIDTH,
            transcendentals=0,
        ),
        name="logits_early",
    )(meta, normed, *near[:NEAR])
    return pl.pallas_call(
        logits_kernel,
        in_specs=[SMEM, VMEM, VMEM, VMEM, *[VMEM] * (9 - NEAR)],
        out_specs=[VMEM, VMEM],
        out_shape=[
            jax.ShapeDtypeStruct((SPAN, LIVE), F32),
            jax.ShapeDtypeStruct((4, LIVE), F32),
        ],
        compiler_params=params(),
        name="logits",
    )(meta, normed, label, first, *near[NEAR:])


def back_kernel(meta_ref, stats_ref, logits_ref, label_ref, layer_ref, *rest):
    *refs, part_ref, row_ref, loss_ref = rest
    stats = stats_ref[...]
    peaks = [stats[:, 4 * c, :] for c in range(2)]
    peak = jnp.max(jnp.maximum(peaks[0], peaks[1]), axis=0, keepdims=True)
    mass = mean = aimed = jnp.zeros((1, LIVE), F32)
    for c in range(2):
        weight = jnp.exp(peaks[c] - peak)
        own = stats[:, 4 * c + 1, :]
        mass += jnp.sum(weight * own, axis=0, keepdims=True)
        moved = stats[:, 4 * c + 2, :] + (peaks[c] - peak) * own
        mean += jnp.sum(weight * moved, axis=0, keepdims=True)
        aimed += jnp.sum(stats[:, 4 * c + 3, :], axis=0, keepdims=True)
    row_ref[...] = mean / mass + (peak - aimed)
    loss = jnp.log(mass) + (peak - aimed)
    for layer in range(2):
        mine = (layer_ref[...] == layer).astype(F32)
        total = jnp.sum(loss * mine, axis=1, keepdims=True)
        loss_ref[layer : layer + 1, :] = total / jnp.sum(mine, axis=1, keepdims=True)
    logits = logits_ref[...]
    column = lax.broadcasted_iota(jnp.int32, (SPAN, LIVE), 0)
    hits = (column + meta_ref[0] == label_ref[...]).astype(F32)
    slope = (jnp.exp(logits - peak) / mass - hits).T.astype(BF16)
    for place in range(8):
        shard = meta_ref[2 + place]
        if place < 7:
            part = jnp.dot(slope, refs[place][...], preferred_element_type=F32)
        else:
            part = jnp.dot(slope[:, :PART], refs[7][...], preferred_element_type=F32)
            part += jnp.dot(slope[:, PART:], refs[8][...], preferred_element_type=F32)
        part_ref[shard] = part.astype(BF16)


def local_back(meta, stats, logits, label, layer, near):
    return pl.pallas_call(
        back_kernel,
        in_specs=[SMEM, VMEM, VMEM, VMEM, VMEM, *[VMEM] * 9],
        out_specs=[VMEM] * 3,
        out_shape=[
            jax.ShapeDtypeStruct((8, LIVE, WIDTH), BF16),
            jax.ShapeDtypeStruct((1, LIVE), F32),
            jax.ShapeDtypeStruct((2, 1), F32),
        ],
        compiler_params=params(),
        name="back",
    )(meta, stats, logits, label, layer, *near)


def spread(values, axes, count):
    copies = jnp.broadcast_to(values[None], (count, *values.shape))
    return lax.all_to_all(copies, axes, 0, 0, tiled=True)


def ring(own):
    up = [(i, (i + 1) % 8) for i in range(8)]
    down = [(i, (i - 1) % 8) for i in range(8)]
    right = left = own
    near = [own]
    for _ in range(3):
        right = lax.ppermute(right, "z", up)
        left = lax.ppermute(left, "z", down)
        near += [right, left]
    near.append(lax.ppermute(right[:PART], "z", up))
    near.append(lax.ppermute(left[PART:], "z", down))
    return near


def body(hidden, gain, head, exit_slots, targets):
    layers, row_dev, part_width = hidden.shape
    most = exit_slots.shape[1]
    own = layers * most
    width = gain.shape[0]
    half = part_width // 2
    z, y, c, x = (lax.axis_index(name) for name in ("z", "y", "c", "x"))
    shards = [lax.rem(z + s, 8) for s in (0, 7, 1, 6, 2, 5, 3, 4)]
    first = ((y * 2 + c) * 4 + x) * SPAN
    meta = jnp.stack([first, c, *shards]).astype(jnp.int32)
    near = ring(head.T)

    packed = pick(exit_slots, targets, hidden)
    picked = packed[:, :part_width]
    pair = lax.all_gather(packed, "c", axis=0, tiled=True)
    pair_half = lax.dynamic_slice_in_dim(pair, c * half, half, 1)
    slots = jnp.concatenate([pair_half, pair[:, part_width:]], axis=1)
    slots = spread(slots, "y", 8).reshape(16 * own, half + 128)

    total = slots.shape[0]
    flag = slots[:, half].astype(F32)
    below = (jnp.arange(total)[:, None] < jnp.arange(total)[None, :]).astype(F32)
    rank = jnp.sum(below * flag[:, None], axis=0)
    place = (rank[None, :] == jnp.arange(LIVE, dtype=F32)[:, None]) & (flag > 0)[None, :]
    place = place.astype(BF16)
    place_out = jnp.pad(place.reshape(LIVE, 16, own), ((0, 0), (0, 0), (0, 16 - own)))
    place_out = place_out.reshape(LIVE, 256)
    compact = jnp.dot(place, slots, preferred_element_type=F32)
    fact = compact[:, half : half + 4].astype(jnp.int32).T
    label_row = (fact[1] * 256 + fact[2]).reshape(1, LIVE)
    layer_row = fact[3].reshape(1, LIVE)
    rows = spread(compact[:, :half].astype(BF16), "x", 4)
    rows = lax.all_gather(rows, "c", axis=0)

    values = rows.astype(F32)
    scale = lax.rsqrt(jnp.sum(values * values, axis=(0, 1, 3)) / width + EPS)
    gain_f = gain.astype(F32)
    gain_rows = gain_f.reshape(4, 2, 1, half).transpose(1, 0, 2, 3)
    normed = (values * scale[:, None] * gain_rows).astype(BF16)

    logits, stats = local_logits(meta, normed, label_row, near)
    stats = lax.all_gather(stats, "c", axis=0, tiled=True)
    stats = spread(stats, ("y", "x"), 32)
    part, gap, group_loss = local_back(meta, stats, logits, label_row, layer_row, near)

    part = lax.all_to_all(part, ("x", "c"), 0, 0, tiled=True)
    part = jnp.sum(part.astype(F32), axis=0).astype(BF16)
    sent = lax.dot_general(place_out, part, (((0,), (0,)), ((), ())), preferred_element_type=F32)
    sent = sent.astype(BF16).reshape(16, 16, half)
    back = lax.all_to_all(sent, ("y", "c"), 0, 0, tiled=True)
    back = jnp.sum(back.reshape(8, 2, 16, half).astype(F32), axis=0)[:, :own]

    gain_own = lax.dynamic_slice_in_dim(gain_f, x * part_width, part_width)
    mine = lax.dynamic_slice_in_dim(place, (y * 2 + c) * own, own, 1).astype(F32)
    scale_own = jnp.sum(mine * scale[:, None], axis=0)
    shift_own = jnp.sum(mine * (scale**2 * gap[0] / width)[:, None], axis=0)
    value_own = picked.reshape(own, 2, half).transpose(1, 0, 2).astype(F32)
    grads = scale_own[:, None] * gain_own.reshape(2, 1, half) * back - value_own * shift_own[:, None]
    exit_grads = grads.astype(BF16).transpose(1, 0, 2).reshape(layers, most, part_width)
    return exit_grads, group_loss


def solution(mesh):
    split = Mesh(mesh.devices.reshape(8, 8, 2, 4), ("z", "y", "c", "x"))
    in_specs = (
        P(None, ("z", "y", "c"), "x"),
        P(),
        P("z", ("y", "c", "x")),
        P(None, ("z", "y", "c")),
        P(("z", "y", "c")),
    )
    out_specs = (P(None, ("z", "y", "c"), "x"), P(None, "z"))
    return jax.shard_map(body, mesh=split, in_specs=in_specs, out_specs=out_specs, check_vma=False)
```

```python
import functools

import jax
import jax.numpy as jnp
from jax import lax
from jax.experimental import pallas as pl
from jax.experimental.pallas import tpu as pltpu
from jax.sharding import Mesh, PartitionSpec as P

EPS = 1e-05
LIVE = 72
SPAN = 500
RING = 3
WIDTH = 640
FACTS = 128
F32 = jnp.float32
BF16 = jnp.bfloat16


def params(mib=32):
    return pltpu.CompilerParams(vmem_limit_bytes=mib * 1024 * 1024)


def pick_kernel(slots_ref, targets_ref, hidden_ref, out_ref, rows, total, sem):
    layers, most = slots_ref.shape
    part_width = hidden_ref.shape[2]
    copies = []
    for i in range(layers * most):
        row = jnp.minimum(slots_ref[i // most, i % most], hidden_ref.shape[1] - 1)
        block = pl.ds(pl.multiple_of((row // 16) * 16, 16), 16)
        copies.append(pltpu.make_async_copy(hidden_ref.at[i // most, block], rows.at[i], sem.at[i]))
        copies[-1].start()
    lane = lax.broadcasted_iota(jnp.int32, (1, FACTS), 1)
    sub = lax.broadcasted_iota(jnp.int32, (16, 1), 0)
    for i, copy in enumerate(copies):
        entry = slots_ref[i // most, i % most]
        row = jnp.minimum(entry, hidden_ref.shape[1] - 1)
        live = (entry < hidden_ref.shape[1]).astype(jnp.int32)
        label = targets_ref[row] * live
        fact = jnp.where(lane == 0, live, 0) + jnp.where(lane == 1, label // 256, 0)
        fact += jnp.where(lane == 2, label % 256, 0) + jnp.where(lane == 3, i // most, 0)
        total[i : i + 1, part_width:] = fact.astype(F32)
        copy.wait()
        mine = (sub == row % 16) & (live > 0)
        picked = jnp.sum(jnp.where(mine, rows[i].astype(F32), 0.0), axis=0, keepdims=True)
        total[i : i + 1, :part_width] = picked
    out_ref[...] = total[...].astype(BF16)


def pick(slots, targets, hidden):
    own, part_width = slots.size, hidden.shape[2]
    return pl.pallas_call(
        pick_kernel,
        in_specs=[SMEM, SMEM, pl.BlockSpec(memory_space=pltpu.HBM)],
        out_specs=VMEM,
        out_shape=jax.ShapeDtypeStruct((own, part_width + FACTS), BF16),
        scratch_shapes=[
            pltpu.VMEM((own, 16, part_width), BF16),
            pltpu.VMEM((own, part_width + FACTS), F32),
            pltpu.SemaphoreType.DMA((own,)),
        ],
        compiler_params=params(56),
        name="pick",
    )(slots, targets, hidden)


def scores(shard, normed_ref, head):
    normed = normed_ref[lax.rem(shard, 2), shard // 2]
    return lax.dot_general(head, normed, (((1,), (1,)), ((), ())), preferred_element_type=F32)


def early_kernel(meta_ref, normed_ref, *rest):
    *refs, logits_ref = rest
    mine = other = jnp.zeros((SPAN, LIVE), F32)
    for i, ref in enumerate(refs):
        part = scores(meta_ref[2 + (i + 1) // 2], normed_ref, ref[...])
        if i == 0 or i % 2 == 1:
            mine += part
        else:
            other += part
    logits_ref[0] = mine
    logits_ref[1] = other


def far_kernel(meta_ref, normed_ref, begun_ref, far_ref, logits_ref):
    logits_ref[0] = begun_ref[0] + scores(meta_ref[2 + RING + 1], normed_ref, far_ref[...])
    logits_ref[1] = begun_ref[1]


def sum_kernel(meta_ref, label_ref, own_ref, came_ref, logits_ref, stats_ref):
    column = lax.broadcasted_iota(jnp.int32, (SPAN, LIVE), 0)
    parts = [own_ref[i] + came_ref[1 - i] for i in range(2)]
    peak = jnp.max(jnp.maximum(*parts), axis=0, keepdims=True)
    mass = mean = aimed = jnp.zeros((1, LIVE), F32)
    for i, logits in enumerate(parts):
        logits_ref[i] = logits
        hits = column + meta_ref[i] == label_ref[...]
        shifted = jnp.exp(logits - peak)
        mass += jnp.sum(shifted, axis=0, keepdims=True)
        mean += jnp.sum(shifted * (logits - peak), axis=0, keepdims=True)
        aimed += jnp.sum(jnp.where(hits, logits, 0.0), axis=0, keepdims=True)
    for i, value in enumerate((peak, mass, mean, aimed)):
        stats_ref[i : i + 1, :] = value


VMEM = pl.BlockSpec(memory_space=pltpu.VMEM)
SMEM = pl.BlockSpec(memory_space=pltpu.SMEM)


BOTH = jax.ShapeDtypeStruct((2, SPAN, LIVE), F32)


def early_logits(meta, normed, near):
    count = len(near)
    return pl.pallas_call(
        early_kernel,
        in_specs=[SMEM, *[VMEM] * (1 + count)],
        out_specs=VMEM,
        out_shape=BOTH,
        compiler_params=params(),
        cost_estimate=pl.CostEstimate(
            flops=2 * count * SPAN * LIVE * WIDTH,
            bytes_accessed=2 * count * SPAN * WIDTH,
            transcendentals=0,
        ),
        name="logits_early",
    )(meta, normed, *near)


def far_logits(meta, normed, begun, far):
    return pl.pallas_call(
        far_kernel,
        in_specs=[SMEM, VMEM, VMEM, VMEM],
        out_specs=VMEM,
        out_shape=BOTH,
        compiler_params=params(),
        name="logits_far",
    )(meta, normed, begun, far)


def sum_logits(meta, label, own, came):
    return pl.pallas_call(
        sum_kernel,
        in_specs=[SMEM, VMEM, VMEM, VMEM],
        out_specs=[VMEM, VMEM],
        out_shape=[BOTH, jax.ShapeDtypeStruct((4, LIVE), F32)],
        compiler_params=params(),
        name="logits",
    )(meta, label, own, came)


def slope_of(logits, first, label, peak, mass):
    column = lax.broadcasted_iota(jnp.int32, (SPAN, LIVE), 0)
    hits = (column + first == label).astype(F32)
    return (jnp.exp(logits - peak) / mass - hits).T.astype(BF16)


def back_kernel(meta_ref, stats_ref, logits_ref, label_ref, layer_ref, *rest):
    *refs, part_ref, row_ref, loss_ref = rest
    stats = stats_ref[...]
    peaks, own = stats[:, 0, :], stats[:, 1, :]
    peak = jnp.max(peaks, axis=0, keepdims=True)
    weight = jnp.exp(peaks - peak)
    mass = jnp.sum(weight * own, axis=0, keepdims=True)
    mean = jnp.sum(weight * (stats[:, 2, :] + (peaks - peak) * own), axis=0, keepdims=True)
    aimed = jnp.sum(stats[:, 3, :], axis=0, keepdims=True)
    row_ref[...] = mean / mass + (peak - aimed)
    loss = jnp.log(mass) + (peak - aimed)
    for layer in range(2):
        mine = (layer_ref[...] == layer).astype(F32)
        total = jnp.sum(loss * mine, axis=1, keepdims=True)
        loss_ref[layer : layer + 1, :] = total / jnp.sum(mine, axis=1, keepdims=True)
    label = label_ref[...]
    mine = slope_of(logits_ref[0], meta_ref[0], label, peak, mass)
    other = slope_of(logits_ref[1], meta_ref[1], label, peak, mass)
    part_ref[...] = jnp.zeros_like(part_ref)
    for place in range(RING + 2):
        own = 0 if place == 0 else 2 * place - 1
        part = jnp.dot(mine, refs[own][...], preferred_element_type=F32)
        if 0 < place <= RING:
            part += jnp.dot(other, refs[own + 1][...], preferred_element_type=F32)
        part_ref[meta_ref[2 + place]] = part.astype(BF16)


def local_back(meta, stats, logits, label, layer, near):
    return pl.pallas_call(
        back_kernel,
        in_specs=[SMEM, *[VMEM] * (4 + len(near))],
        out_specs=[VMEM] * 3,
        out_shape=[
            jax.ShapeDtypeStruct((8, LIVE, WIDTH), BF16),
            jax.ShapeDtypeStruct((1, LIVE), F32),
            jax.ShapeDtypeStruct((2, 1), F32),
        ],
        compiler_params=params(),
        name="back",
    )(meta, stats, logits, label, layer, *near)


def spread(values, axes, count):
    copies = jnp.broadcast_to(values[None], (count, *values.shape))
    return lax.all_to_all(copies, axes, 0, 0, tiled=True)


def swap_core(values):
    return lax.ppermute(values, "c", [(0, 1), (1, 0)])


def after(values, *others):
    return lax.optimization_barrier((values, *others))[0]


def ring(own):
    onward = [(2 * i + c, 2 * ((i + 1 - 2 * c) % 8) + c) for i in range(8) for c in range(2)]
    mine = own
    other = swapped = swap_core(own)
    near = [own]
    for _ in range(RING):
        mine = lax.ppermute(mine, ("z", "c"), onward)
        other = lax.ppermute(other, ("z", "c"), onward)
        near += [mine, other]
    return swapped, [*near, lax.ppermute(mine, ("z", "c"), onward)]


def body(hidden, gain, head, exit_slots, targets):
    layers, row_dev, part_width = hidden.shape
    most = exit_slots.shape[1]
    own = layers * most
    width = gain.shape[0]
    half = part_width // 2
    z, y, c, x = (lax.axis_index(name) for name in ("z", "y", "c", "x"))
    shards = [lax.rem(z + 8 + (2 * c - 1) * s, 8) for s in range(RING + 2)]
    first = ((y * 2 + c) * 4 + x) * SPAN
    first_other = ((y * 2 + 1 - c) * 4 + x) * SPAN
    meta = jnp.stack([first, first_other, *shards]).astype(jnp.int32)
    swapped, near = ring(head.T)

    packed = pick(exit_slots, targets, hidden)
    picked = packed[:, :part_width]
    pair = lax.all_gather(packed, "c", axis=0, tiled=True)
    pair_half = lax.dynamic_slice_in_dim(pair, c * half, half, 1)
    slots = jnp.concatenate([pair_half, pair[:, part_width:]], axis=1)
    slots = after(slots, near[1], near[2])
    slots = spread(slots, "y", 8).reshape(16 * own, half + 128)

    slots = after(slots, near[3], near[4])
    total = slots.shape[0]
    flag = slots[:, half].astype(F32)
    below = (jnp.arange(total)[:, None] < jnp.arange(total)[None, :]).astype(F32)
    rank = jnp.sum(below * flag[:, None], axis=0)
    place = (rank[None, :] == jnp.arange(LIVE, dtype=F32)[:, None]) & (flag > 0)[None, :]
    place = place.astype(BF16)
    place_out = jnp.pad(place.reshape(LIVE, 16, own), ((0, 0), (0, 0), (0, 16 - own)))
    place_out = place_out.reshape(LIVE, 256)
    compact = jnp.dot(place, slots, preferred_element_type=F32)
    fact = compact[:, half : half + 4].astype(jnp.int32).T
    label_row = (fact[1] * 256 + fact[2]).reshape(1, LIVE)
    layer_row = fact[3].reshape(1, LIVE)
    rows = spread(compact[:, :half].astype(BF16), "x", 4)
    rows = after(rows, near[5], near[6])
    rows = lax.all_gather(rows, "c", axis=0)

    values = rows.astype(F32)
    scale = lax.rsqrt(jnp.sum(values * values, axis=(0, 1, 3)) / width + EPS)
    gain_f = gain.astype(F32)
    gain_rows = gain_f.reshape(4, 2, 1, half).transpose(1, 0, 2, 3)
    normed = (values * scale[:, None] * gain_rows).astype(BF16)

    logits = early_logits(meta, normed, near[:-1])
    logits = far_logits(meta, normed, logits, near[-1])
    logits, stats = sum_logits(meta, label_row, logits, swap_core(logits))
    stats = spread(stats, ("y", "x"), 32)
    part, gap, group_loss = local_back(meta, stats, logits, label_row, layer_row, near)

    part = lax.all_to_all(part, ("x", "c"), 0, 0, tiled=True)
    part = jnp.sum(part.astype(F32), axis=0).astype(BF16)
    sent = lax.dot_general(place_out, part, (((0,), (0,)), ((), ())), preferred_element_type=F32)
    sent = sent.astype(BF16).reshape(16, 16, half)
    back = lax.all_to_all(sent, ("y", "c"), 0, 0, tiled=True)
    back = jnp.sum(back.reshape(8, 2, 16, half).astype(F32), axis=0)[:, :own]

    gain_own = lax.dynamic_slice_in_dim(gain_f, x * part_width, part_width)
    mine = lax.dynamic_slice_in_dim(place, (y * 2 + c) * own, own, 1).astype(F32)
    scale_own = jnp.sum(mine * scale[:, None], axis=0)
    shift_own = jnp.sum(mine * (scale**2 * gap[0] / width)[:, None], axis=0)
    value_own = picked.reshape(own, 2, half).transpose(1, 0, 2).astype(F32)
    grads = scale_own[:, None] * gain_own.reshape(2, 1, half) * back - value_own * shift_own[:, None]
    exit_grads = grads.astype(BF16).transpose(1, 0, 2).reshape(layers, most, part_width)
    return exit_grads, group_loss


def solution(mesh):
    split = Mesh(mesh.devices.reshape(8, 8, 2, 4), ("z", "y", "c", "x"))
    in_specs = (
        P(None, ("z", "y", "c"), "x"),
        P(),
        P("z", ("y", "c", "x")),
        P(None, ("z", "y", "c")),
        P(("z", "y", "c")),
    )
    out_specs = (P(None, ("z", "y", "c"), "x"), P(None, "z"))
    return jax.shard_map(body, mesh=split, in_specs=in_specs, out_specs=out_specs, check_vma=False)
```

```python
import functools

import jax
import jax.numpy as jnp
from jax import lax
from jax.experimental import pallas as pl
from jax.experimental.pallas import tpu as pltpu
from jax.sharding import Mesh, PartitionSpec as P

EPS = 1e-05
LIVE = 72
SPAN = 500
RING = 3
WIDTH = 640
FACTS = 128
F32 = jnp.float32
BF16 = jnp.bfloat16


def params(mib=32):
    return pltpu.CompilerParams(vmem_limit_bytes=mib * 1024 * 1024)


def pick_kernel(slots_ref, targets_ref, hidden_ref, out_ref, rows, total, sem):
    layers, most = slots_ref.shape
    part_width = hidden_ref.shape[2]
    copies = []
    for i in range(layers * most):
        row = jnp.minimum(slots_ref[i // most, i % most], hidden_ref.shape[1] - 1)
        block = pl.ds(pl.multiple_of((row // 16) * 16, 16), 16)
        copies.append(pltpu.make_async_copy(hidden_ref.at[i // most, block], rows.at[i], sem.at[i]))
        copies[-1].start()
    lane = lax.broadcasted_iota(jnp.int32, (1, FACTS), 1)
    sub = lax.broadcasted_iota(jnp.int32, (16, 1), 0)
    for i, copy in enumerate(copies):
        entry = slots_ref[i // most, i % most]
        row = jnp.minimum(entry, hidden_ref.shape[1] - 1)
        live = (entry < hidden_ref.shape[1]).astype(jnp.int32)
        label = targets_ref[row] * live
        fact = jnp.where(lane == 0, live, 0) + jnp.where(lane == 1, label // 256, 0)
        fact += jnp.where(lane == 2, label % 256, 0) + jnp.where(lane == 3, i // most, 0)
        total[i : i + 1, part_width:] = fact.astype(F32)
        copy.wait()
        mine = (sub == row % 16) & (live > 0)
        picked = jnp.sum(jnp.where(mine, rows[i].astype(F32), 0.0), axis=0, keepdims=True)
        total[i : i + 1, :part_width] = picked
    out_ref[...] = total[...].astype(BF16)


def pick(slots, targets, hidden):
    own, part_width = slots.size, hidden.shape[2]
    return pl.pallas_call(
        pick_kernel,
        in_specs=[SMEM, SMEM, pl.BlockSpec(memory_space=pltpu.HBM)],
        out_specs=VMEM,
        out_shape=jax.ShapeDtypeStruct((own, part_width + FACTS), BF16),
        scratch_shapes=[
            pltpu.VMEM((own, 16, part_width), BF16),
            pltpu.VMEM((own, part_width + FACTS), F32),
            pltpu.SemaphoreType.DMA((own,)),
        ],
        compiler_params=params(56),
        name="pick",
    )(slots, targets, hidden)


def scores(shard, normed_ref, head):
    normed = normed_ref[lax.rem(shard, 2), shard // 2]
    return lax.dot_general(head, normed, (((1,), (1,)), ((), ())), preferred_element_type=F32)


def early_kernel(meta_ref, normed_ref, *rest):
    *refs, mine_ref, other_ref = rest
    mine = other = jnp.zeros((SPAN, LIVE), F32)
    for i, ref in enumerate(refs):
        part = scores(meta_ref[2 + (i + 1) // 2], normed_ref, ref[...])
        if i == 0 or i % 2 == 1:
            mine += part
        else:
            other += part
    mine_ref[...] = mine
    other_ref[...] = other


def far_kernel(meta_ref, normed_ref, begun_ref, far_ref, logits_ref):
    logits_ref[...] = begun_ref[...] + scores(meta_ref[2 + RING + 1], normed_ref, far_ref[...])


def sum_kernel(meta_ref, label_ref, mine_ref, more_ref, other_ref, rest_ref, logits_ref, stats_ref):
    column = lax.broadcasted_iota(jnp.int32, (SPAN, LIVE), 0)
    parts = [mine_ref[...] + more_ref[...], other_ref[...] + rest_ref[...]]
    peak = jnp.max(jnp.maximum(*parts), axis=0, keepdims=True)
    mass = mean = aimed = jnp.zeros((1, LIVE), F32)
    for i, logits in enumerate(parts):
        logits_ref[i] = logits
        hits = column + meta_ref[i] == label_ref[...]
        shifted = jnp.exp(logits - peak)
        mass += jnp.sum(shifted, axis=0, keepdims=True)
        mean += jnp.sum(shifted * (logits - peak), axis=0, keepdims=True)
        aimed += jnp.sum(jnp.where(hits, logits, 0.0), axis=0, keepdims=True)
    for i, value in enumerate((peak, mass, mean, aimed)):
        stats_ref[i : i + 1, :] = value


VMEM = pl.BlockSpec(memory_space=pltpu.VMEM)
SMEM = pl.BlockSpec(memory_space=pltpu.SMEM)


ONE = jax.ShapeDtypeStruct((SPAN, LIVE), F32)
BOTH = jax.ShapeDtypeStruct((2, SPAN, LIVE), F32)


def early_logits(meta, normed, near):
    count = len(near)
    return pl.pallas_call(
        early_kernel,
        in_specs=[SMEM, *[VMEM] * (1 + count)],
        out_specs=[VMEM, VMEM],
        out_shape=[ONE, ONE],
        compiler_params=params(),
        cost_estimate=pl.CostEstimate(
            flops=2 * count * SPAN * LIVE * WIDTH,
            bytes_accessed=2 * count * SPAN * WIDTH,
            transcendentals=0,
        ),
        name="logits_early",
    )(meta, normed, *near)


def far_logits(meta, normed, begun, far):
    return pl.pallas_call(
        far_kernel,
        in_specs=[SMEM, VMEM, VMEM, VMEM],
        out_specs=VMEM,
        out_shape=ONE,
        compiler_params=params(),
        name="logits_far",
    )(meta, normed, begun, far)


def sum_logits(meta, label, mine, more, other, rest):
    return pl.pallas_call(
        sum_kernel,
        in_specs=[SMEM, *[VMEM] * 5],
        out_specs=[VMEM, VMEM],
        out_shape=[BOTH, jax.ShapeDtypeStruct((4, LIVE), F32)],
        compiler_params=params(),
        name="logits",
    )(meta, label, mine, more, other, rest)


def slope_of(logits, first, label, peak, mass):
    column = lax.broadcasted_iota(jnp.int32, (SPAN, LIVE), 0)
    hits = (column + first == label).astype(F32)
    return (jnp.exp(logits - peak) / mass - hits).T.astype(BF16)


def back_kernel(meta_ref, stats_ref, logits_ref, label_ref, layer_ref, *rest):
    *refs, part_ref, row_ref, loss_ref = rest
    stats = stats_ref[...]
    peaks, own = stats[:, 0, :], stats[:, 1, :]
    peak = jnp.max(peaks, axis=0, keepdims=True)
    weight = jnp.exp(peaks - peak)
    mass = jnp.sum(weight * own, axis=0, keepdims=True)
    mean = jnp.sum(weight * (stats[:, 2, :] + (peaks - peak) * own), axis=0, keepdims=True)
    aimed = jnp.sum(stats[:, 3, :], axis=0, keepdims=True)
    row_ref[...] = mean / mass + (peak - aimed)
    loss = jnp.log(mass) + (peak - aimed)
    for layer in range(2):
        mine = (layer_ref[...] == layer).astype(F32)
        total = jnp.sum(loss * mine, axis=1, keepdims=True)
        loss_ref[layer : layer + 1, :] = total / jnp.sum(mine, axis=1, keepdims=True)
    label = label_ref[...]
    mine = slope_of(logits_ref[0], meta_ref[0], label, peak, mass)
    other = slope_of(logits_ref[1], meta_ref[1], label, peak, mass)
    for i in range(RING):
        part_ref[meta_ref[4 + RING + i]] = jnp.zeros((LIVE, WIDTH), BF16)
    for place in range(RING + 2):
        own = 0 if place == 0 else 2 * place - 1
        part = jnp.dot(mine, refs[own][...], preferred_element_type=F32)
        if 0 < place <= RING:
            part += jnp.dot(other, refs[own + 1][...], preferred_element_type=F32)
        part_ref[meta_ref[2 + place]] = part.astype(BF16)


def local_back(meta, stats, logits, label, layer, near):
    return pl.pallas_call(
        back_kernel,
        in_specs=[SMEM, *[VMEM] * (4 + len(near))],
        out_specs=[VMEM] * 3,
        out_shape=[
            jax.ShapeDtypeStruct((8, LIVE, WIDTH), BF16),
            jax.ShapeDtypeStruct((1, LIVE), F32),
            jax.ShapeDtypeStruct((2, 1), F32),
        ],
        compiler_params=params(),
        name="back",
    )(meta, stats, logits, label, layer, *near)


def spread(values, axes, count):
    copies = jnp.broadcast_to(values[None], (count, *values.shape))
    return lax.all_to_all(copies, axes, 0, 0, tiled=True)


def swap_core(values):
    return lax.ppermute(values, "c", [(0, 1), (1, 0)])


def after(values, *others):
    return lax.optimization_barrier((values, *others))[0]


def ring(own):
    onward = [(2 * i + c, 2 * ((i + 1 - 2 * c) % 8) + c) for i in range(8) for c in range(2)]
    mine = own
    other = swapped = swap_core(own)
    near = [own]
    for _ in range(RING):
        mine = lax.ppermute(mine, ("z", "c"), onward)
        other = lax.ppermute(other, ("z", "c"), onward)
        near += [mine, other]
    return swapped, [*near, lax.ppermute(mine, ("z", "c"), onward)]


def body(hidden, gain, head, exit_slots, targets):
    layers, row_dev, part_width = hidden.shape
    most = exit_slots.shape[1]
    own = layers * most
    width = gain.shape[0]
    half = part_width // 2
    z, y, c, x = (lax.axis_index(name) for name in ("z", "y", "c", "x"))
    shards = [lax.rem(z + 8 + (2 * c - 1) * s, 8) for s in range(RING + 2)]
    first = ((y * 2 + c) * 4 + x) * SPAN
    first_other = ((y * 2 + 1 - c) * 4 + x) * SPAN
    absent = [lax.rem(z + 8 - (2 * c - 1) * s, 8) for s in range(1, RING + 1)]
    meta = jnp.stack([first, first_other, *shards, *absent]).astype(jnp.int32)
    swapped, near = ring(head.T)

    packed = pick(exit_slots, targets, hidden)
    picked = packed[:, :part_width]
    pair = lax.all_gather(packed, "c", axis=0, tiled=True)
    pair_half = lax.dynamic_slice_in_dim(pair, c * half, half, 1)
    slots = jnp.concatenate([pair_half, pair[:, part_width:]], axis=1)
    slots = after(slots, near[1], near[2])
    slots = spread(slots, "y", 8).reshape(16 * own, half + 128)

    slots = after(slots, near[3], near[4])
    total = slots.shape[0]
    flag = slots[:, half].astype(F32)
    below = (jnp.arange(total)[:, None] < jnp.arange(total)[None, :]).astype(F32)
    rank = jnp.sum(below * flag[:, None], axis=0)
    place = (rank[None, :] == jnp.arange(LIVE, dtype=F32)[:, None]) & (flag > 0)[None, :]
    place = place.astype(BF16)
    place_out = jnp.pad(place.reshape(LIVE, 16, own), ((0, 0), (0, 0), (0, 16 - own)))
    place_out = place_out.reshape(LIVE, 256)
    compact = jnp.dot(place, slots, preferred_element_type=F32)
    fact = compact[:, half : half + 4].astype(jnp.int32).T
    label_row = (fact[1] * 256 + fact[2]).reshape(1, LIVE)
    layer_row = fact[3].reshape(1, LIVE)
    rows = spread(compact[:, :half].astype(BF16), "x", 4)
    rows = after(rows, near[5], near[6])
    rows = lax.all_gather(rows, "c", axis=0)

    values = rows.astype(F32)
    scale = lax.rsqrt(jnp.sum(values * values, axis=(0, 1, 3)) / width + EPS)
    gain_f = gain.astype(F32)
    gain_rows = gain_f.reshape(4, 2, 1, half).transpose(1, 0, 2, 3)
    normed = (values * scale[:, None] * gain_rows).astype(BF16)

    mine, other = early_logits(meta, normed, near[:-1])
    more = swap_core(other)
    mine = far_logits(meta, normed, mine, near[-1])
    logits, stats = sum_logits(meta, label_row, mine, more, other, swap_core(mine))
    stats = spread(stats, ("y", "x"), 32)
    part, gap, group_loss = local_back(meta, stats, logits, label_row, layer_row, near)

    part = lax.all_to_all(part, ("x", "c"), 0, 0, tiled=True)
    part = jnp.sum(part.astype(F32), axis=0).astype(BF16)
    sent = lax.dot_general(place_out, part, (((0,), (0,)), ((), ())), preferred_element_type=F32)
    sent = sent.astype(BF16).reshape(16, 16, half)
    back = lax.all_to_all(sent, ("y", "c"), 0, 0, tiled=True)
    back = jnp.sum(back.reshape(8, 2, 16, half).astype(F32), axis=0)[:, :own]

    gain_own = lax.dynamic_slice_in_dim(gain_f, x * part_width, part_width)
    mine = lax.dynamic_slice_in_dim(place, (y * 2 + c) * own, own, 1).astype(F32)
    scale_own = jnp.sum(mine * scale[:, None], axis=0)
    shift_own = jnp.sum(mine * (scale**2 * gap[0] / width)[:, None], axis=0)
    value_own = picked.reshape(own, 2, half).transpose(1, 0, 2).astype(F32)
    grads = scale_own[:, None] * gain_own.reshape(2, 1, half) * back - value_own * shift_own[:, None]
    exit_grads = grads.astype(BF16).transpose(1, 0, 2).reshape(layers, most, part_width)
    return exit_grads, group_loss


def solution(mesh):
    split = Mesh(mesh.devices.reshape(8, 8, 2, 4), ("z", "y", "c", "x"))
    in_specs = (
        P(None, ("z", "y", "c"), "x"),
        P(),
        P("z", ("y", "c", "x")),
        P(None, ("z", "y", "c")),
        P(("z", "y", "c")),
    )
    out_specs = (P(None, ("z", "y", "c"), "x"), P(None, "z"))
    return jax.shard_map(body, mesh=split, in_specs=in_specs, out_specs=out_specs, check_vma=False)
```

```python
import functools

import jax
import jax.numpy as jnp
from jax import lax
from jax.experimental import pallas as pl
from jax.experimental.pallas import tpu as pltpu
from jax.sharding import Mesh, PartitionSpec as P

EPS = 1e-05
LIVE = 72
SPAN = 500
RING = 3
WIDTH = 640
FACTS = 128
F32 = jnp.float32
BF16 = jnp.bfloat16


def params(mib=32):
    return pltpu.CompilerParams(vmem_limit_bytes=mib * 1024 * 1024)


def pick_kernel(slots_ref, targets_ref, hidden_ref, out_ref, rows, total, sem):
    layers, most = slots_ref.shape
    part_width = hidden_ref.shape[2]
    copies = []
    for i in range(layers * most):
        row = jnp.minimum(slots_ref[i // most, i % most], hidden_ref.shape[1] - 1)
        block = pl.ds(pl.multiple_of((row // 16) * 16, 16), 16)
        copies.append(pltpu.make_async_copy(hidden_ref.at[i // most, block], rows.at[i], sem.at[i]))
        copies[-1].start()
    lane = lax.broadcasted_iota(jnp.int32, (1, FACTS), 1)
    sub = lax.broadcasted_iota(jnp.int32, (16, 1), 0)
    for i, copy in enumerate(copies):
        entry = slots_ref[i // most, i % most]
        row = jnp.minimum(entry, hidden_ref.shape[1] - 1)
        live = (entry < hidden_ref.shape[1]).astype(jnp.int32)
        label = targets_ref[row] * live
        fact = jnp.where(lane == 0, live, 0) + jnp.where(lane == 1, label // 256, 0)
        fact += jnp.where(lane == 2, label % 256, 0) + jnp.where(lane == 3, i // most, 0)
        total[i : i + 1, part_width:] = fact.astype(F32)
        copy.wait()
        mine = (sub == row % 16) & (live > 0)
        picked = jnp.sum(jnp.where(mine, rows[i].astype(F32), 0.0), axis=0, keepdims=True)
        total[i : i + 1, :part_width] = picked
    out_ref[...] = total[...].astype(BF16)


def pick(slots, targets, hidden):
    own, part_width = slots.size, hidden.shape[2]
    return pl.pallas_call(
        pick_kernel,
        in_specs=[SMEM, SMEM, pl.BlockSpec(memory_space=pltpu.HBM)],
        out_specs=VMEM,
        out_shape=jax.ShapeDtypeStruct((own, part_width + FACTS), BF16),
        scratch_shapes=[
            pltpu.VMEM((own, 16, part_width), BF16),
            pltpu.VMEM((own, part_width + FACTS), F32),
            pltpu.SemaphoreType.DMA((own,)),
        ],
        compiler_params=params(56),
        name="pick",
    )(slots, targets, hidden)


def compact_kernel(slots_ref, rows_ref, place_ref, label_ref, layer_ref):
    total, lanes = slots_ref.shape
    half = lanes - FACTS
    facts = slots_ref[:, half:].astype(F32).T
    flag = facts[0:1, :]
    below = lax.broadcasted_iota(jnp.int32, (total, total), 0)
    below = (below < lax.broadcasted_iota(jnp.int32, (total, total), 1)).astype(F32)
    rank = jnp.dot(flag, below, preferred_element_type=F32)
    row = lax.broadcasted_iota(jnp.int32, (LIVE, total), 0)
    place = ((row == rank.astype(jnp.int32)) & (flag > 0)).astype(F32).astype(BF16)
    place_ref[...] = place
    rows = jnp.dot(place, slots_ref[:, :half], preferred_element_type=F32).astype(BF16)
    for i in range(rows_ref.shape[0]):
        rows_ref[i] = rows
    known = lax.dot_general(
        facts[0:8, :].astype(BF16), place, (((1,), (1,)), ((), ())), preferred_element_type=F32
    ).astype(jnp.int32)
    label_ref[...] = known[1:2, :] * 256 + known[2:3, :]
    layer_ref[...] = known[3:4, :]


def compact(slots):
    total, lanes = slots.shape
    return pl.pallas_call(
        compact_kernel,
        in_specs=[VMEM],
        out_specs=[VMEM] * 4,
        out_shape=[
            jax.ShapeDtypeStruct((4, LIVE, lanes - FACTS), BF16),
            jax.ShapeDtypeStruct((LIVE, total), BF16),
            jax.ShapeDtypeStruct((1, LIVE), jnp.int32),
            jax.ShapeDtypeStruct((1, LIVE), jnp.int32),
        ],
        compiler_params=params(),
        name="compact",
    )(slots)


def scores(shard, normed_ref, head):
    normed = normed_ref[lax.rem(shard, 2), shard // 2]
    return lax.dot_general(head, normed, (((1,), (1,)), ((), ())), preferred_element_type=F32)


def early_kernel(meta_ref, normed_ref, *rest):
    *refs, mine_ref, other_ref = rest
    mine = other = jnp.zeros((SPAN, LIVE), F32)
    for i, ref in enumerate(refs):
        part = scores(meta_ref[2 + (i + 1) // 2], normed_ref, ref[...])
        if i == 0 or i % 2 == 1:
            mine += part
        else:
            other += part
    mine_ref[...] = mine
    other_ref[...] = other


def far_kernel(meta_ref, normed_ref, begun_ref, far_ref, logits_ref):
    logits_ref[...] = begun_ref[...] + scores(meta_ref[2 + RING + 1], normed_ref, far_ref[...])


def sum_kernel(meta_ref, label_ref, mine_ref, more_ref, other_ref, rest_ref, logits_ref, stats_ref):
    column = lax.broadcasted_iota(jnp.int32, (SPAN, LIVE), 0)
    parts = [mine_ref[...] + more_ref[...], other_ref[...] + rest_ref[...]]
    peak = jnp.max(jnp.maximum(*parts), axis=0, keepdims=True)
    mass = mean = aimed = jnp.zeros((1, LIVE), F32)
    for i, logits in enumerate(parts):
        logits_ref[i] = logits
        hits = column + meta_ref[i] == label_ref[...]
        shifted = jnp.exp(logits - peak)
        mass += jnp.sum(shifted, axis=0, keepdims=True)
        mean += jnp.sum(shifted * (logits - peak), axis=0, keepdims=True)
        aimed += jnp.sum(jnp.where(hits, logits, 0.0), axis=0, keepdims=True)
    for i, value in enumerate((peak, mass, mean, aimed)):
        stats_ref[i : i + 1, :] = value


VMEM = pl.BlockSpec(memory_space=pltpu.VMEM)
SMEM = pl.BlockSpec(memory_space=pltpu.SMEM)


ONE = jax.ShapeDtypeStruct((SPAN, LIVE), F32)
BOTH = jax.ShapeDtypeStruct((2, SPAN, LIVE), F32)


def early_logits(meta, normed, near):
    count = len(near)
    return pl.pallas_call(
        early_kernel,
        in_specs=[SMEM, *[VMEM] * (1 + count)],
        out_specs=[VMEM, VMEM],
        out_shape=[ONE, ONE],
        compiler_params=params(),
        cost_estimate=pl.CostEstimate(
            flops=2 * count * SPAN * LIVE * WIDTH,
            bytes_accessed=2 * count * SPAN * WIDTH,
            transcendentals=0,
        ),
        name="logits_early",
    )(meta, normed, *near)


def far_logits(meta, normed, begun, far):
    return pl.pallas_call(
        far_kernel,
        in_specs=[SMEM, VMEM, VMEM, VMEM],
        out_specs=VMEM,
        out_shape=ONE,
        compiler_params=params(),
        name="logits_far",
    )(meta, normed, begun, far)


def sum_logits(meta, label, mine, more, other, rest):
    return pl.pallas_call(
        sum_kernel,
        in_specs=[SMEM, *[VMEM] * 5],
        out_specs=[VMEM, VMEM],
        out_shape=[BOTH, jax.ShapeDtypeStruct((4, LIVE), F32)],
        compiler_params=params(),
        name="logits",
    )(meta, label, mine, more, other, rest)


def slope_of(logits, first, label, peak, mass):
    column = lax.broadcasted_iota(jnp.int32, (SPAN, LIVE), 0)
    hits = (column + first == label).astype(F32)
    return (jnp.exp(logits - peak) / mass - hits).T.astype(BF16)


def back_kernel(meta_ref, stats_ref, logits_ref, label_ref, layer_ref, *rest):
    *refs, part_ref, row_ref, loss_ref = rest
    stats = stats_ref[...]
    peaks, own = stats[:, 0, :], stats[:, 1, :]
    peak = jnp.max(peaks, axis=0, keepdims=True)
    weight = jnp.exp(peaks - peak)
    mass = jnp.sum(weight * own, axis=0, keepdims=True)
    mean = jnp.sum(weight * (stats[:, 2, :] + (peaks - peak) * own), axis=0, keepdims=True)
    aimed = jnp.sum(stats[:, 3, :], axis=0, keepdims=True)
    row_ref[...] = mean / mass + (peak - aimed)
    loss = jnp.log(mass) + (peak - aimed)
    for layer in range(2):
        mine = (layer_ref[...] == layer).astype(F32)
        total = jnp.sum(loss * mine, axis=1, keepdims=True)
        loss_ref[layer : layer + 1, :] = total / jnp.sum(mine, axis=1, keepdims=True)
    label = label_ref[...]
    mine = slope_of(logits_ref[0], meta_ref[0], label, peak, mass)
    other = slope_of(logits_ref[1], meta_ref[1], label, peak, mass)
    for i in range(RING):
        part_ref[meta_ref[4 + RING + i]] = jnp.zeros((LIVE, WIDTH), BF16)
    for place in range(RING + 2):
        own = 0 if place == 0 else 2 * place - 1
        part = jnp.dot(mine, refs[own][...], preferred_element_type=F32)
        if 0 < place <= RING:
            part += jnp.dot(other, refs[own + 1][...], preferred_element_type=F32)
        part_ref[meta_ref[2 + place]] = part.astype(BF16)


def local_back(meta, stats, logits, label, layer, near):
    return pl.pallas_call(
        back_kernel,
        in_specs=[SMEM, *[VMEM] * (4 + len(near))],
        out_specs=[VMEM] * 3,
        out_shape=[
            jax.ShapeDtypeStruct((8, LIVE, WIDTH), BF16),
            jax.ShapeDtypeStruct((1, LIVE), F32),
            jax.ShapeDtypeStruct((2, 1), F32),
        ],
        compiler_params=params(),
        name="back",
    )(meta, stats, logits, label, layer, *near)


def spread(values, axes, count):
    copies = jnp.broadcast_to(values[None], (count, *values.shape))
    return lax.all_to_all(copies, axes, 0, 0, tiled=True)


def swap_core(values):
    return lax.ppermute(values, "c", [(0, 1), (1, 0)])


def after(values, *others):
    return lax.optimization_barrier((values, *others))[0]


def onward(values):
    pairs = [(2 * i + c, 2 * ((i + 1 - 2 * c) % 8) + c) for i in range(8) for c in range(2)]
    return lax.ppermute(values, ("z", "c"), pairs)


def ring(own, swapped, first):
    mine, other = onward(own), onward(swapped)
    near = [own, mine, other]
    mine = after(mine, first)
    for _ in range(RING - 1):
        mine, other = onward(mine), onward(other)
        near += [mine, other]
    return [*near, onward(mine)]


def body(hidden, gain, head, exit_slots, targets):
    layers, row_dev, part_width = hidden.shape
    most = exit_slots.shape[1]
    own = layers * most
    width = gain.shape[0]
    half = part_width // 2
    z, y, c, x = (lax.axis_index(name) for name in ("z", "y", "c", "x"))
    shards = [lax.rem(z + 8 + (2 * c - 1) * s, 8) for s in range(RING + 2)]
    first = ((y * 2 + c) * 4 + x) * SPAN
    first_other = ((y * 2 + 1 - c) * 4 + x) * SPAN
    absent = [lax.rem(z + 8 - (2 * c - 1) * s, 8) for s in range(1, RING + 1)]
    meta = jnp.stack([first, first_other, *shards, *absent]).astype(jnp.int32)
    packed = pick(exit_slots, targets, hidden)
    picked = packed[:, :part_width]
    pair = lax.all_gather(packed, "c", axis=0, tiled=True)
    near = ring(head.T, swap_core(head.T), pair)
    pair_half = lax.dynamic_slice_in_dim(pair, c * half, half, 1)
    slots = jnp.concatenate([pair_half, pair[:, part_width:]], axis=1)
    slots = after(slots, near[1], near[2])
    slots = spread(slots, "y", 8).reshape(16 * own, half + 128)

    slots = after(slots, near[3], near[4])
    rows, place, label_row, layer_row = compact(slots)
    place_out = jnp.pad(place.reshape(LIVE, 16, own), ((0, 0), (0, 0), (0, 16 - own)))
    place_out = place_out.reshape(LIVE, 256)
    rows = lax.all_to_all(rows, "x", 0, 0, tiled=True)
    rows = after(rows, near[5], near[6])
    rows = lax.all_gather(rows, "c", axis=0)

    values = rows.astype(F32)
    scale = lax.rsqrt(jnp.sum(values * values, axis=(0, 1, 3)) / width + EPS)
    gain_f = gain.astype(F32)
    gain_rows = gain_f.reshape(4, 2, 1, half).transpose(1, 0, 2, 3)
    normed = (values * scale[:, None] * gain_rows).astype(BF16)

    mine, other = early_logits(meta, normed, near[:-1])
    more = swap_core(other)
    mine = far_logits(meta, normed, mine, near[-1])
    logits, stats = sum_logits(meta, label_row, mine, more, other, swap_core(mine))
    stats = spread(stats, ("y", "x"), 32)
    part, gap, group_loss = local_back(meta, stats, logits, label_row, layer_row, near)

    part = lax.all_to_all(part, ("x", "c"), 0, 0, tiled=True)
    part = jnp.sum(part.astype(F32), axis=0).astype(BF16)
    sent = lax.dot_general(place_out, part, (((0,), (0,)), ((), ())), preferred_element_type=F32)
    sent = sent.astype(BF16).reshape(16, 16, half)
    back = lax.all_to_all(sent, ("y", "c"), 0, 0, tiled=True)
    back = jnp.sum(back.reshape(8, 2, 16, half).astype(F32), axis=0)[:, :own]

    gain_own = lax.dynamic_slice_in_dim(gain_f, x * part_width, part_width)
    mine = lax.dynamic_slice_in_dim(place, (y * 2 + c) * own, own, 1).astype(F32)
    scale_own = jnp.sum(mine * scale[:, None], axis=0)
    shift_own = jnp.sum(mine * (scale**2 * gap[0] / width)[:, None], axis=0)
    value_own = picked.reshape(own, 2, half).transpose(1, 0, 2).astype(F32)
    grads = scale_own[:, None] * gain_own.reshape(2, 1, half) * back - value_own * shift_own[:, None]
    exit_grads = grads.astype(BF16).transpose(1, 0, 2).reshape(layers, most, part_width)
    return exit_grads, group_loss


def solution(mesh):
    split = Mesh(mesh.devices.reshape(8, 8, 2, 4), ("z", "y", "c", "x"))
    in_specs = (
        P(None, ("z", "y", "c"), "x"),
        P(),
        P("z", ("y", "c", "x")),
        P(None, ("z", "y", "c")),
        P(("z", "y", "c")),
    )
    out_specs = (P(None, ("z", "y", "c"), "x"), P(None, "z"))
    return jax.shard_map(body, mesh=split, in_specs=in_specs, out_specs=out_specs, check_vma=False)
```

```python
import functools

import jax
import jax.numpy as jnp
from jax import lax
from jax.experimental import pallas as pl
from jax.experimental.pallas import tpu as pltpu
from jax.sharding import Mesh, PartitionSpec as P

EPS = 1e-05
LIVE = 72
SPAN = 500
RING = 3
WIDTH = 640
FACTS = 128
F32 = jnp.float32
BF16 = jnp.bfloat16


def params(mib=32):
    return pltpu.CompilerParams(vmem_limit_bytes=mib * 1024 * 1024)


def pick_kernel(slots_ref, targets_ref, hidden_ref, out_ref, rows, total, sem):
    layers, most = slots_ref.shape
    part_width = hidden_ref.shape[2]
    copies = []
    for i in range(layers * most):
        row = jnp.minimum(slots_ref[i // most, i % most], hidden_ref.shape[1] - 1)
        block = pl.ds(pl.multiple_of((row // 16) * 16, 16), 16)
        copies.append(pltpu.make_async_copy(hidden_ref.at[i // most, block], rows.at[i], sem.at[i]))
        copies[-1].start()
    lane = lax.broadcasted_iota(jnp.int32, (1, FACTS), 1)
    sub = lax.broadcasted_iota(jnp.int32, (16, 1), 0)
    for i, copy in enumerate(copies):
        entry = slots_ref[i // most, i % most]
        row = jnp.minimum(entry, hidden_ref.shape[1] - 1)
        live = (entry < hidden_ref.shape[1]).astype(jnp.int32)
        label = targets_ref[row] * live
        fact = jnp.where(lane == 0, live, 0) + jnp.where(lane == 1, label // 256, 0)
        fact += jnp.where(lane == 2, label % 256, 0) + jnp.where(lane == 3, i // most, 0)
        total[i : i + 1, part_width:] = fact.astype(F32)
        copy.wait()
        mine = (sub == row % 16) & (live > 0)
        picked = jnp.sum(jnp.where(mine, rows[i].astype(F32), 0.0), axis=0, keepdims=True)
        total[i : i + 1, :part_width] = picked
    out_ref[...] = total[...].astype(BF16)


def pick(slots, targets, hidden):
    own, part_width = slots.size, hidden.shape[2]
    return pl.pallas_call(
        pick_kernel,
        in_specs=[SMEM, SMEM, pl.BlockSpec(memory_space=pltpu.HBM)],
        out_specs=VMEM,
        out_shape=jax.ShapeDtypeStruct((own, part_width + FACTS), BF16),
        scratch_shapes=[
            pltpu.VMEM((own, 16, part_width), BF16),
            pltpu.VMEM((own, part_width + FACTS), F32),
            pltpu.SemaphoreType.DMA((own,)),
        ],
        compiler_params=params(56),
        name="pick",
    )(slots, targets, hidden)


def compact_kernel(slots_ref, rows_ref, place_ref, label_ref, layer_ref):
    total, lanes = slots_ref.shape
    half = lanes - FACTS
    facts = slots_ref[:, half:].astype(F32).T
    flag = facts[0:1, :]
    below = lax.broadcasted_iota(jnp.int32, (total, total), 0)
    below = (below < lax.broadcasted_iota(jnp.int32, (total, total), 1)).astype(F32)
    rank = jnp.dot(flag, below, preferred_element_type=F32)
    row = lax.broadcasted_iota(jnp.int32, (LIVE, total), 0)
    place = ((row == rank.astype(jnp.int32)) & (flag > 0)).astype(F32).astype(BF16)
    place_ref[...] = place
    rows = jnp.dot(place, slots_ref[:, :half], preferred_element_type=F32).astype(BF16)
    for i in range(rows_ref.shape[0]):
        rows_ref[i] = rows
    known = lax.dot_general(
        facts[0:8, :].astype(BF16), place, (((1,), (1,)), ((), ())), preferred_element_type=F32
    ).astype(jnp.int32)
    label_ref[...] = known[1:2, :] * 256 + known[2:3, :]
    layer_ref[...] = known[3:4, :]


def compact(slots):
    total, lanes = slots.shape
    return pl.pallas_call(
        compact_kernel,
        in_specs=[VMEM],
        out_specs=[VMEM] * 4,
        out_shape=[
            jax.ShapeDtypeStruct((4, LIVE, lanes - FACTS), BF16),
            jax.ShapeDtypeStruct((LIVE, total), BF16),
            jax.ShapeDtypeStruct((1, LIVE), jnp.int32),
            jax.ShapeDtypeStruct((1, LIVE), jnp.int32),
        ],
        compiler_params=params(),
        name="compact",
    )(slots)


def scores(shard, normed_ref, head):
    normed = normed_ref[lax.rem(shard, 2), shard // 2]
    return lax.dot_general(head, normed, (((1,), (1,)), ((), ())), preferred_element_type=F32)


def early_kernel(meta_ref, normed_ref, *rest):
    *refs, mine_ref, other_ref = rest
    mine = other = jnp.zeros((SPAN, LIVE), F32)
    for i, ref in enumerate(refs):
        part = scores(meta_ref[2 + (i + 1) // 2], normed_ref, ref[...])
        if i == 0 or i % 2 == 1:
            mine += part
        else:
            other += part
    mine_ref[...] = mine
    other_ref[...] = other


def far_kernel(meta_ref, normed_ref, begun_ref, far_ref, logits_ref):
    logits_ref[...] = begun_ref[...] + scores(meta_ref[2 + RING + 1], normed_ref, far_ref[...])


def sum_kernel(meta_ref, label_ref, mine_ref, more_ref, other_ref, rest_ref, logits_ref, stats_ref):
    column = lax.broadcasted_iota(jnp.int32, (SPAN, LIVE), 0)
    parts = [mine_ref[...] + more_ref[...], other_ref[...] + rest_ref[...]]
    peak = jnp.max(jnp.maximum(*parts), axis=0, keepdims=True)
    mass = mean = aimed = jnp.zeros((1, LIVE), F32)
    for i, logits in enumerate(parts):
        logits_ref[i] = logits
        hits = column + meta_ref[i] == label_ref[...]
        shifted = jnp.exp(logits - peak)
        mass += jnp.sum(shifted, axis=0, keepdims=True)
        mean += jnp.sum(shifted * (logits - peak), axis=0, keepdims=True)
        aimed += jnp.sum(jnp.where(hits, logits, 0.0), axis=0, keepdims=True)
    for i, value in enumerate((peak, mass, mean, aimed)):
        stats_ref[i : i + 1, :] = value


VMEM = pl.BlockSpec(memory_space=pltpu.VMEM)
SMEM = pl.BlockSpec(memory_space=pltpu.SMEM)


ONE = jax.ShapeDtypeStruct((SPAN, LIVE), F32)
BOTH = jax.ShapeDtypeStruct((2, SPAN, LIVE), F32)


def early_logits(meta, normed, near):
    count = len(near)
    return pl.pallas_call(
        early_kernel,
        in_specs=[SMEM, *[VMEM] * (1 + count)],
        out_specs=[VMEM, VMEM],
        out_shape=[ONE, ONE],
        compiler_params=params(),
        cost_estimate=pl.CostEstimate(
            flops=2 * count * SPAN * LIVE * WIDTH,
            bytes_accessed=2 * count * SPAN * WIDTH,
            transcendentals=0,
        ),
        name="logits_early",
    )(meta, normed, *near)


def far_logits(meta, normed, begun, far):
    return pl.pallas_call(
        far_kernel,
        in_specs=[SMEM, VMEM, VMEM, VMEM],
        out_specs=VMEM,
        out_shape=ONE,
        compiler_params=params(),
        name="logits_far",
    )(meta, normed, begun, far)


def sum_logits(meta, label, mine, more, other, rest):
    return pl.pallas_call(
        sum_kernel,
        in_specs=[SMEM, *[VMEM] * 5],
        out_specs=[VMEM, VMEM],
        out_shape=[BOTH, jax.ShapeDtypeStruct((4, LIVE), F32)],
        compiler_params=params(),
        name="logits",
    )(meta, label, mine, more, other, rest)


def slope_of(logits, first, label, peak, mass):
    column = lax.broadcasted_iota(jnp.int32, (SPAN, LIVE), 0)
    hits = (column + first == label).astype(F32)
    return (jnp.exp(logits - peak) / mass - hits).T.astype(BF16)


def back_kernel(meta_ref, stats_ref, logits_ref, label_ref, layer_ref, *rest):
    *refs, part_ref, row_ref, loss_ref = rest
    stats = stats_ref[...]
    peaks, own = stats[:, 0, :], stats[:, 1, :]
    peak = jnp.max(peaks, axis=0, keepdims=True)
    weight = jnp.exp(peaks - peak)
    mass = jnp.sum(weight * own, axis=0, keepdims=True)
    mean = jnp.sum(weight * (stats[:, 2, :] + (peaks - peak) * own), axis=0, keepdims=True)
    aimed = jnp.sum(stats[:, 3, :], axis=0, keepdims=True)
    row_ref[...] = mean / mass + (peak - aimed)
    loss = jnp.log(mass) + (peak - aimed)
    for layer in range(2):
        mine = (layer_ref[...] == layer).astype(F32)
        total = jnp.sum(loss * mine, axis=1, keepdims=True)
        loss_ref[layer : layer + 1, :] = total / jnp.sum(mine, axis=1, keepdims=True)
    label = label_ref[...]
    mine = slope_of(logits_ref[0], meta_ref[0], label, peak, mass)
    other = slope_of(logits_ref[1], meta_ref[1], label, peak, mass)
    for i in range(RING):
        part_ref[meta_ref[4 + RING + i]] = jnp.zeros((LIVE, WIDTH), BF16)
    for place in range(RING + 2):
        own = 0 if place == 0 else 2 * place - 1
        part = jnp.dot(mine, refs[own][...], preferred_element_type=F32)
        if 0 < place <= RING:
            part += jnp.dot(other, refs[own + 1][...], preferred_element_type=F32)
        part_ref[meta_ref[2 + place]] = part.astype(BF16)


def local_back(meta, stats, logits, label, layer, near):
    return pl.pallas_call(
        back_kernel,
        in_specs=[SMEM, *[VMEM] * (4 + len(near))],
        out_specs=[VMEM] * 3,
        out_shape=[
            jax.ShapeDtypeStruct((8, LIVE, WIDTH), BF16),
            jax.ShapeDtypeStruct((1, LIVE), F32),
            jax.ShapeDtypeStruct((2, 1), F32),
        ],
        compiler_params=params(),
        name="back",
    )(meta, stats, logits, label, layer, *near)


def spread(values, axes, count):
    copies = jnp.broadcast_to(values[None], (count, *values.shape))
    return lax.all_to_all(copies, axes, 0, 0, tiled=True)


def swap_core(values):
    return lax.ppermute(values, "c", [(0, 1), (1, 0)])


def after(values, *others):
    return lax.optimization_barrier((values, *others))[0]


def onward(values):
    pairs = [(2 * i + c, 2 * ((i + 1 - 2 * c) % 8) + c) for i in range(8) for c in range(2)]
    return lax.ppermute(values, ("z", "c"), pairs)


def ring(own, swapped, first):
    mine, other = onward(own), onward(swapped)
    near = [own, mine, other]
    mine = after(mine, first)
    for _ in range(RING - 1):
        mine, other = onward(mine), onward(other)
        near += [mine, other]
    return [*near, onward(mine)]


def body(hidden, gain, head, exit_slots, targets):
    layers, row_dev, part_width = hidden.shape
    most = exit_slots.shape[1]
    own = layers * most
    width = gain.shape[0]
    half = part_width // 2
    z, y, c, x = (lax.axis_index(name) for name in ("z", "y", "c", "x"))
    shards = [lax.rem(z + 8 + (2 * c - 1) * s, 8) for s in range(RING + 2)]
    first = ((y * 2 + c) * 4 + x) * SPAN
    first_other = ((y * 2 + 1 - c) * 4 + x) * SPAN
    absent = [lax.rem(z + 8 - (2 * c - 1) * s, 8) for s in range(1, RING + 1)]
    meta = jnp.stack([first, first_other, *shards, *absent]).astype(jnp.int32)
    packed = pick(exit_slots, targets, hidden)
    picked = packed[:, :part_width]
    pair = lax.all_gather(packed, "c", axis=0, tiled=True)
    near = ring(head.T, swap_core(head.T), pair)
    pair_half = lax.dynamic_slice_in_dim(pair, c * half, half, 1)
    slots = jnp.concatenate([pair_half, pair[:, part_width:]], axis=1)
    slots = after(slots, near[1], near[2])
    slots = spread(slots, "y", 8).reshape(16 * own, half + 128)

    slots = after(slots, near[3], near[4])
    rows, place, label_row, layer_row = compact(slots)
    place_out = jnp.pad(place.reshape(LIVE, 16, own), ((0, 0), (0, 0), (0, 16 - own)))
    place_out = place_out.reshape(LIVE, 256)
    rows = lax.all_to_all(rows, "x", 0, 0, tiled=True)
    rows = after(rows, near[5], near[6])
    rows = lax.all_gather(rows, "c", axis=0)

    values = rows.astype(F32)
    scale = lax.rsqrt(jnp.sum(values * values, axis=(0, 1, 3)) / width + EPS)
    gain_f = gain.astype(F32)
    gain_rows = gain_f.reshape(4, 2, 1, half).transpose(1, 0, 2, 3)
    normed = (values * scale[:, None] * gain_rows).astype(BF16)

    mine, other = early_logits(meta, normed, near[:-1])
    more = swap_core(other)
    mine = far_logits(meta, normed, mine, near[-1])
    more, mine = lax.optimization_barrier((more, mine))
    logits, stats = sum_logits(meta, label_row, mine, more, other, swap_core(mine))
    stats = spread(stats, ("y", "x"), 32)
    part, gap, group_loss = local_back(meta, stats, logits, label_row, layer_row, near)

    part = lax.all_to_all(part, ("x", "c"), 0, 0, tiled=True)
    part = jnp.sum(part.astype(F32), axis=0).astype(BF16)
    sent = lax.dot_general(place_out, part, (((0,), (0,)), ((), ())), preferred_element_type=F32)
    sent = sent.astype(BF16).reshape(16, 16, half)
    back = lax.all_to_all(sent, ("y", "c"), 0, 0, tiled=True)
    back = jnp.sum(back.reshape(8, 2, 16, half).astype(F32), axis=0)[:, :own]

    gain_own = lax.dynamic_slice_in_dim(gain_f, x * part_width, part_width)
    mine = lax.dynamic_slice_in_dim(place, (y * 2 + c) * own, own, 1).astype(F32)
    scale_own = jnp.sum(mine * scale[:, None], axis=0)
    shift_own = jnp.sum(mine * (scale**2 * gap[0] / width)[:, None], axis=0)
    value_own = picked.reshape(own, 2, half).transpose(1, 0, 2).astype(F32)
    grads = scale_own[:, None] * gain_own.reshape(2, 1, half) * back - value_own * shift_own[:, None]
    exit_grads = grads.astype(BF16).transpose(1, 0, 2).reshape(layers, most, part_width)
    return exit_grads, group_loss


def solution(mesh):
    split = Mesh(mesh.devices.reshape(8, 8, 2, 4), ("z", "y", "c", "x"))
    in_specs = (
        P(None, ("z", "y", "c"), "x"),
        P(),
        P("z", ("y", "c", "x")),
        P(None, ("z", "y", "c")),
        P(("z", "y", "c")),
    )
    out_specs = (P(None, ("z", "y", "c"), "x"), P(None, "z"))
    return jax.shard_map(body, mesh=split, in_specs=in_specs, out_specs=out_specs, check_vma=False)
```

```python
import functools

import jax
import jax.numpy as jnp
from jax import lax
from jax.experimental import pallas as pl
from jax.experimental.pallas import tpu as pltpu
from jax.sharding import Mesh, PartitionSpec as P

EPS = 1e-05
LIVE = 72
SPAN = 500
RING = 3
WIDTH = 640
FACTS = 128
F32 = jnp.float32
BF16 = jnp.bfloat16


def params(mib=32):
    return pltpu.CompilerParams(vmem_limit_bytes=mib * 1024 * 1024)


def pick_kernel(slots_ref, targets_ref, hidden_ref, out_ref, rows, total, sem):
    layers, most = slots_ref.shape
    part_width = hidden_ref.shape[2]
    copies = []
    for i in range(layers * most):
        row = jnp.minimum(slots_ref[i // most, i % most], hidden_ref.shape[1] - 1)
        block = pl.ds(pl.multiple_of((row // 16) * 16, 16), 16)
        copies.append(pltpu.make_async_copy(hidden_ref.at[i // most, block], rows.at[i], sem.at[i]))
        copies[-1].start()
    lane = lax.broadcasted_iota(jnp.int32, (1, FACTS), 1)
    sub = lax.broadcasted_iota(jnp.int32, (16, 1), 0)
    for i, copy in enumerate(copies):
        entry = slots_ref[i // most, i % most]
        row = jnp.minimum(entry, hidden_ref.shape[1] - 1)
        live = (entry < hidden_ref.shape[1]).astype(jnp.int32)
        label = targets_ref[row] * live
        fact = jnp.where(lane == 0, live, 0) + jnp.where(lane == 1, label // 256, 0)
        fact += jnp.where(lane == 2, label % 256, 0) + jnp.where(lane == 3, i // most, 0)
        total[i : i + 1, part_width:] = fact.astype(F32)
        copy.wait()
        mine = (sub == row % 16) & (live > 0)
        picked = jnp.sum(jnp.where(mine, rows[i].astype(F32), 0.0), axis=0, keepdims=True)
        total[i : i + 1, :part_width] = picked
    out_ref[...] = total[...].astype(BF16)


def pick(slots, targets, hidden):
    own, part_width = slots.size, hidden.shape[2]
    return pl.pallas_call(
        pick_kernel,
        in_specs=[SMEM, SMEM, pl.BlockSpec(memory_space=pltpu.HBM)],
        out_specs=VMEM,
        out_shape=jax.ShapeDtypeStruct((own, part_width + FACTS), BF16),
        scratch_shapes=[
            pltpu.VMEM((own, 16, part_width), BF16),
            pltpu.VMEM((own, part_width + FACTS), F32),
            pltpu.SemaphoreType.DMA((own,)),
        ],
        compiler_params=params(56),
        name="pick",
    )(slots, targets, hidden)


def compact_kernel(slots_ref, rows_ref, place_ref, label_ref, layer_ref):
    total, lanes = slots_ref.shape
    half = lanes - FACTS
    facts = slots_ref[:, half:].astype(F32).T
    flag = facts[0:1, :]
    below = lax.broadcasted_iota(jnp.int32, (total, total), 0)
    below = (below < lax.broadcasted_iota(jnp.int32, (total, total), 1)).astype(F32)
    rank = jnp.dot(flag, below, preferred_element_type=F32)
    row = lax.broadcasted_iota(jnp.int32, (LIVE, total), 0)
    place = ((row == rank.astype(jnp.int32)) & (flag > 0)).astype(F32).astype(BF16)
    place_ref[...] = place
    rows = jnp.dot(place, slots_ref[:, :half], preferred_element_type=F32).astype(BF16)
    for i in range(rows_ref.shape[0]):
        rows_ref[i] = rows
    known = lax.dot_general(
        facts[0:8, :].astype(BF16), place, (((1,), (1,)), ((), ())), preferred_element_type=F32
    ).astype(jnp.int32)
    label_ref[...] = known[1:2, :] * 256 + known[2:3, :]
    layer_ref[...] = known[3:4, :]


def compact(slots):
    total, lanes = slots.shape
    return pl.pallas_call(
        compact_kernel,
        in_specs=[VMEM],
        out_specs=[VMEM] * 4,
        out_shape=[
            jax.ShapeDtypeStruct((4, LIVE, lanes - FACTS), BF16),
            jax.ShapeDtypeStruct((LIVE, total), BF16),
            jax.ShapeDtypeStruct((1, LIVE), jnp.int32),
            jax.ShapeDtypeStruct((1, LIVE), jnp.int32),
        ],
        compiler_params=params(56),
        name="compact",
    )(slots)


def scores(shard, normed_ref, head):
    normed = normed_ref[lax.rem(shard, 2), shard // 2]
    return lax.dot_general(head, normed, (((1,), (1,)), ((), ())), preferred_element_type=F32)


def early_kernel(meta_ref, normed_ref, *rest):
    *refs, mine_ref, other_ref = rest
    mine = other = jnp.zeros((SPAN, LIVE), F32)
    for i, ref in enumerate(refs):
        part = scores(meta_ref[2 + (i + 1) // 2], normed_ref, ref[...])
        if i == 0 or i % 2 == 1:
            mine += part
        else:
            other += part
    mine_ref[...] = mine
    other_ref[...] = other


def far_kernel(meta_ref, normed_ref, begun_ref, far_ref, logits_ref):
    logits_ref[...] = begun_ref[...] + scores(meta_ref[2 + RING + 1], normed_ref, far_ref[...])


def sum_kernel(meta_ref, label_ref, mine_ref, more_ref, other_ref, rest_ref, logits_ref, stats_ref):
    column = lax.broadcasted_iota(jnp.int32, (SPAN, LIVE), 0)
    parts = [mine_ref[...] + more_ref[...], other_ref[...] + rest_ref[...]]
    peak = jnp.max(jnp.maximum(*parts), axis=0, keepdims=True)
    mass = mean = aimed = jnp.zeros((1, LIVE), F32)
    for i, logits in enumerate(parts):
        logits_ref[i] = logits
        hits = column + meta_ref[i] == label_ref[...]
        shifted = jnp.exp(logits - peak)
        mass += jnp.sum(shifted, axis=0, keepdims=True)
        mean += jnp.sum(shifted * (logits - peak), axis=0, keepdims=True)
        aimed += jnp.sum(jnp.where(hits, logits, 0.0), axis=0, keepdims=True)
    for i, value in enumerate((peak, mass, mean, aimed)):
        stats_ref[i : i + 1, :] = value


VMEM = pl.BlockSpec(memory_space=pltpu.VMEM)
SMEM = pl.BlockSpec(memory_space=pltpu.SMEM)


ONE = jax.ShapeDtypeStruct((SPAN, LIVE), F32)
BOTH = jax.ShapeDtypeStruct((2, SPAN, LIVE), F32)


def early_logits(meta, normed, near):
    count = len(near)
    return pl.pallas_call(
        early_kernel,
        in_specs=[SMEM, *[VMEM] * (1 + count)],
        out_specs=[VMEM, VMEM],
        out_shape=[ONE, ONE],
        compiler_params=params(),
        cost_estimate=pl.CostEstimate(
            flops=2 * count * SPAN * LIVE * WIDTH,
            bytes_accessed=2 * count * SPAN * WIDTH,
            transcendentals=0,
        ),
        name="logits_early",
    )(meta, normed, *near)


def far_logits(meta, normed, begun, far):
    return pl.pallas_call(
        far_kernel,
        in_specs=[SMEM, VMEM, VMEM, VMEM],
        out_specs=VMEM,
        out_shape=ONE,
        compiler_params=params(),
        name="logits_far",
    )(meta, normed, begun, far)


def sum_logits(meta, label, mine, more, other, rest):
    return pl.pallas_call(
        sum_kernel,
        in_specs=[SMEM, *[VMEM] * 5],
        out_specs=[VMEM, VMEM],
        out_shape=[BOTH, jax.ShapeDtypeStruct((4, LIVE), F32)],
        compiler_params=params(),
        name="logits",
    )(meta, label, mine, more, other, rest)


def slope_of(logits, first, label, peak, mass):
    column = lax.broadcasted_iota(jnp.int32, (SPAN, LIVE), 0)
    hits = (column + first == label).astype(F32)
    return (jnp.exp(logits - peak) / mass - hits).T.astype(BF16)


def back_kernel(meta_ref, stats_ref, logits_ref, label_ref, layer_ref, *rest):
    *refs, part_ref, row_ref, loss_ref = rest
    stats = stats_ref[...]
    peaks, own = stats[:, 0, :], stats[:, 1, :]
    peak = jnp.max(peaks, axis=0, keepdims=True)
    weight = jnp.exp(peaks - peak)
    mass = jnp.sum(weight * own, axis=0, keepdims=True)
    mean = jnp.sum(weight * (stats[:, 2, :] + (peaks - peak) * own), axis=0, keepdims=True)
    aimed = jnp.sum(stats[:, 3, :], axis=0, keepdims=True)
    row_ref[...] = mean / mass + (peak - aimed)
    loss = jnp.log(mass) + (peak - aimed)
    for layer in range(2):
        mine = (layer_ref[...] == layer).astype(F32)
        total = jnp.sum(loss * mine, axis=1, keepdims=True)
        loss_ref[layer : layer + 1, :] = total / jnp.sum(mine, axis=1, keepdims=True)
    label = label_ref[...]
    mine = slope_of(logits_ref[0], meta_ref[0], label, peak, mass)
    other = slope_of(logits_ref[1], meta_ref[1], label, peak, mass)
    for i in range(RING):
        part_ref[meta_ref[4 + RING + i]] = jnp.zeros((LIVE, WIDTH), BF16)
    for place in range(RING + 2):
        own = 0 if place == 0 else 2 * place - 1
        part = jnp.dot(mine, refs[own][...], preferred_element_type=F32)
        if 0 < place <= RING:
            part += jnp.dot(other, refs[own + 1][...], preferred_element_type=F32)
        part_ref[meta_ref[2 + place]] = part.astype(BF16)


def local_back(meta, stats, logits, label, layer, near):
    return pl.pallas_call(
        back_kernel,
        in_specs=[SMEM, *[VMEM] * (4 + len(near))],
        out_specs=[VMEM] * 3,
        out_shape=[
            jax.ShapeDtypeStruct((8, LIVE, WIDTH), BF16),
            jax.ShapeDtypeStruct((1, LIVE), F32),
            jax.ShapeDtypeStruct((2, 1), F32),
        ],
        compiler_params=params(),
        name="back",
    )(meta, stats, logits, label, layer, *near)


def spread(values, axes, count):
    copies = jnp.broadcast_to(values[None], (count, *values.shape))
    return lax.all_to_all(copies, axes, 0, 0, tiled=True)


def swap_core(values):
    return lax.ppermute(values, "c", [(0, 1), (1, 0)])


def after(values, *others):
    return lax.optimization_barrier((values, *others))[0]


def onward(values):
    pairs = [(2 * i + c, 2 * ((i + 1 - 2 * c) % 8) + c) for i in range(8) for c in range(2)]
    return lax.ppermute(values, ("z", "c"), pairs)


def ring(own, swapped, first):
    mine, other = onward(own), onward(swapped)
    near = [own, mine, other]
    mine = after(mine, first)
    for _ in range(RING - 1):
        mine, other = onward(mine), onward(other)
        near += [mine, other]
    return [*near, onward(mine)]


def body(hidden, gain, head, exit_slots, targets):
    layers, row_dev, part_width = hidden.shape
    most = exit_slots.shape[1]
    own = layers * most
    width = gain.shape[0]
    half = part_width // 2
    z, y, c, x = (lax.axis_index(name) for name in ("z", "y", "c", "x"))
    shards = [lax.rem(z + 8 + (2 * c - 1) * s, 8) for s in range(RING + 2)]
    first = ((y * 2 + c) * 4 + x) * SPAN
    first_other = ((y * 2 + 1 - c) * 4 + x) * SPAN
    absent = [lax.rem(z + 8 - (2 * c - 1) * s, 8) for s in range(1, RING + 1)]
    meta = jnp.stack([first, first_other, *shards, *absent]).astype(jnp.int32)
    packed = pick(exit_slots, targets, hidden)
    picked = packed[:, :part_width]
    pair = lax.all_gather(packed, "c", axis=0, tiled=True)
    near = ring(head.T, swap_core(head.T), pair)
    pair_half = lax.dynamic_slice_in_dim(pair, c * half, half, 1)
    slots = jnp.concatenate([pair_half, pair[:, part_width:]], axis=1)
    slots = after(slots, near[1], near[2])
    slots = spread(slots, "y", 8).reshape(16 * own, half + 128)

    slots = after(slots, near[3], near[4])
    rows, place, label_row, layer_row = compact(slots)
    place_out = jnp.pad(place.reshape(LIVE, 16, own), ((0, 0), (0, 0), (0, 16 - own)))
    place_out = place_out.reshape(LIVE, 256)
    rows = lax.all_to_all(rows, "x", 0, 0, tiled=True)
    rows = after(rows, near[5], near[6])
    rows = lax.all_gather(rows, "c", axis=0)

    values = rows.astype(F32)
    scale = lax.rsqrt(jnp.sum(values * values, axis=(0, 1, 3)) / width + EPS)
    gain_f = gain.astype(F32)
    gain_rows = gain_f.reshape(4, 2, 1, half).transpose(1, 0, 2, 3)
    normed = (values * scale[:, None] * gain_rows).astype(BF16)

    mine, other = early_logits(meta, normed, near[:-1])
    more = swap_core(other)
    mine = far_logits(meta, normed, mine, near[-1])
    more, mine = lax.optimization_barrier((more, mine))
    logits, stats = sum_logits(meta, label_row, mine, more, other, swap_core(mine))
    stats = spread(stats, ("y", "x"), 32)
    part, gap, group_loss = local_back(meta, stats, logits, label_row, layer_row, near)

    part = lax.all_to_all(part, ("x", "c"), 0, 0, tiled=True)
    part = jnp.sum(part.astype(F32), axis=0).astype(BF16)
    sent = lax.dot_general(place_out, part, (((0,), (0,)), ((), ())), preferred_element_type=F32)
    sent = sent.astype(BF16).reshape(16, 16, half)
    back = lax.all_to_all(sent, ("y", "c"), 0, 0, tiled=True)
    back = jnp.sum(back.reshape(8, 2, 16, half).astype(F32), axis=0)[:, :own]

    gain_own = lax.dynamic_slice_in_dim(gain_f, x * part_width, part_width)
    mine = lax.dynamic_slice_in_dim(place, (y * 2 + c) * own, own, 1).astype(F32)
    scale_own = jnp.sum(mine * scale[:, None], axis=0)
    shift_own = jnp.sum(mine * (scale**2 * gap[0] / width)[:, None], axis=0)
    value_own = picked.reshape(own, 2, half).transpose(1, 0, 2).astype(F32)
    grads = scale_own[:, None] * gain_own.reshape(2, 1, half) * back - value_own * shift_own[:, None]
    exit_grads = grads.astype(BF16).transpose(1, 0, 2).reshape(layers, most, part_width)
    return exit_grads, group_loss


def solution(mesh):
    split = Mesh(mesh.devices.reshape(8, 8, 2, 4), ("z", "y", "c", "x"))
    in_specs = (
        P(None, ("z", "y", "c"), "x"),
        P(),
        P("z", ("y", "c", "x")),
        P(None, ("z", "y", "c")),
        P(("z", "y", "c")),
    )
    out_specs = (P(None, ("z", "y", "c"), "x"), P(None, "z"))
    return jax.shard_map(body, mesh=split, in_specs=in_specs, out_specs=out_specs, check_vma=False)
```
